256 devices in a mesh: fsdp: 32 (over x, y, core), tp: 8 (over z).
Axes of the slice: x: 4, y: 4, z: 8, core: 2. Of those that a mesh axis runs over, the one named last changes fastest.
Arguments:
- momentum: bfloat16 [2, 28672, 8192], P(None, 'fsdp', 'tp'), may hold values from -200 to 200
- right_factor: bfloat16 [2, 512, 8192], P(None, 'fsdp', 'tp'), may hold values from -6 to 6
Outputs:
- new_momentum: bfloat16 [2, 28672, 8192], P(None, 'fsdp', 'tp')
- update: bfloat16 [2, 28672, 8192], P(None, 'fsdp', 'tp')
- new_factor: bfloat16 [2, 512, 8192], P(None, 'fsdp', 'tp')
The draws below stay inside these ranges and needn't reach their ends.
All inputs are finite; a program needn't handle non-finite values.
Results may differ from the reference program's by a relative error of at most 0.006.
Values may be sent and summed in bfloat16 or wider, within the bound.
A program may use at most 128 MiB of HBM per device.

```python
import math
import jax
import jax.numpy as jnp
from jax import lax

D = 8192
FF = 28672
RANK = 512
LAYERS = 2


def scale_profile(key, count, trend, shape):
    position = jnp.arange(count, dtype=jnp.float32) / count
    rough = jnp.exp(jax.random.uniform(key, shape, jnp.float32, 0.0, math.log(10.0)))
    rising = jnp.exp(math.log(trend) * position).reshape(shape[1:] if shape[0] == 1 and len(shape) == 2 else shape[-2:] if shape[-1] == 1 else shape[-1:])
    rough_mean = 99.0 / (2.0 * math.log(10.0))
    trend_mean = (trend * trend - 1.0) / (2.0 * math.log(trend))
    return rough * rising / math.sqrt(rough_mean * trend_mean)


def draw_momentum(key, part):
    key = jax.random.fold_in(key, 11)
    base_key, row_key, col_key = jax.random.split(key, 3)
    trend = 3.0
    base = jnp.clip(jax.random.normal(base_key, (LAYERS, FF, D), jnp.float32), -6.0, 6.0)
    row_scale = scale_profile(row_key, FF, trend, (LAYERS, FF, 1))
    col_scale = scale_profile(col_key, D, trend, (LAYERS, 1, D))
    return (base * row_scale * col_scale).astype(jnp.bfloat16)


def block_levels(stream_key, dims, pieces, low, largest):
    level = 1.0
    for dim, blocks in pieces:
        draws = jax.random.uniform(jax.random.fold_in(jax.random.fold_in(stream_key, 6), dim), (blocks,), jnp.float32, low / len(pieces), largest / len(pieces))
        level = level * jnp.repeat(jnp.exp(draws), dims[dim] // blocks).reshape((-1,) + (1,) * (len(dims) - 1 - dim))
    return level


def bell_draw(key, shape, width, limit, shards=(), kind=jnp.bfloat16):
    array = width * jax.random.normal(key, shape, jnp.float32)
    if shards:
        array = array * block_levels(key, shape, shards, -0.22, 0.18)
    return jnp.clip(array, -limit, limit).astype(kind)


def setup_inputs(seed: int = 0) -> dict:
    key_list = jax.random.split(jax.random.key(seed), 3)
    momentum = draw_momentum(jax.random.fold_in(key_list[2], 71), 0)
    right_factor = bell_draw(key_list[1], (LAYERS, RANK, D), 1.0, 6.0, ((1, 32), (2, 8)))
    return dict(momentum=momentum, right_factor=right_factor)


def reference(momentum, right_factor):
    highest = lax.Precision.HIGHEST
    scale = math.sqrt(FF * D / RANK)
    moms = []
    updates = []
    factors = []
    for layer in range(LAYERS):
        matrix = momentum[layer]
        factor = right_factor[layer]
        project = jnp.dot(matrix.astype(jnp.float32), factor.T.astype(jnp.float32), preferred_element_type=jnp.float32)
        gram = jnp.dot(project.T, project, precision=highest)
        chol = jnp.linalg.cholesky(gram)
        inverse = lax.linalg.triangular_solve(chol, jnp.eye(RANK, dtype=jnp.float32), left_side=True, lower=True)
        ortho = jnp.dot(project, inverse.T, precision=highest).astype(jnp.bfloat16)
        right = jnp.dot(ortho.T.astype(jnp.float32), matrix.astype(jnp.float32), preferred_element_type=jnp.float32)
        sumsq = lax.optimization_barrier(jnp.sum(right * right, axis=1, keepdims=True))
        normed = (right * lax.rsqrt(sumsq + 1e-06)).astype(jnp.bfloat16)
        right_b = right.astype(jnp.bfloat16)
        feedback = jnp.dot(ortho.astype(jnp.float32), right_b.astype(jnp.float32), preferred_element_type=jnp.float32)
        moms.append((matrix.astype(jnp.float32) - 0.05 * feedback).astype(jnp.bfloat16))
        direction = jnp.dot(ortho.astype(jnp.float32), normed.astype(jnp.float32), preferred_element_type=jnp.float32)
        updates.append((scale * direction).astype(jnp.bfloat16))
        factors.append(normed)
    return (jnp.stack(moms), jnp.stack(updates), jnp.stack(factors))
```

```python
import functools
import math

import jax
import jax.numpy as jnp
from jax import lax
from jax.experimental import pallas as pl
from jax.experimental.pallas import tpu as pltpu
from jax.sharding import PartitionSpec as P

MESH = pl.DeviceIdType.MESH
HI = lax.Precision.HIGHEST
CORES = 2
NB = 128
VMEM_BYTES = 56 * 2**20
F32 = jnp.float32
BF16 = jnp.bfloat16


class Place:
    def __init__(self, side, depth):
        f, self.z = lax.axis_index("fsdp"), lax.axis_index("tp")
        self.side, self.depth = side, depth
        self.x, self.y, self.c = f // (side * CORES), (f // CORES) % side, f % CORES

    def at(self, x=None, y=None, c=None, z=None):
        x = self.x if x is None else x
        y = self.y if y is None else y
        c = self.c if c is None else c
        z = self.z if z is None else z
        return ((x * self.side + y) * CORES + c, z)

    def along(self, axis, t):
        return self.at(x=t) if axis == 0 else self.at(y=t)

    def mine(self, axis):
        return self.x if axis == 0 else self.y

    def others(self, axis):
        return [(o, lax.rem(self.mine(axis) + o, self.side)) for o in range(1, self.side)]

    def others_z(self):
        return [(o, lax.rem(self.z + o, self.depth)) for o in range(1, self.depth)]

    def barrier(self):
        sem = pltpu.get_barrier_semaphore()
        devices = [self.at(c=1 - self.c)]
        devices += [self.along(a, t) for a in (0, 1) for _, t in self.others(a)]
        devices += [self.at(z=t) for _, t in self.others_z()]
        for device in devices:
            pl.semaphore_signal(sem, inc=1, device_id=device, device_id_type=MESH)
        pl.semaphore_wait(sem, len(devices))


class Wire:
    def __init__(self, send, recv):
        self.send, self.recv, self.used, self.copies = send, recv, 0, []

    def put(self, src, dst, device):
        n = self.used
        self.used += 1
        copy = pltpu.make_async_remote_copy(
            src_ref=src,
            dst_ref=dst,
            send_sem=self.send.at[n],
            recv_sem=self.recv.at[n],
            device_id=device,
            device_id_type=MESH,
        )
        copy.start()
        self.copies.append(copy)
        return copy

    def finish(self):
        for copy in self.copies:
            copy.wait_send()


def arrive(copies):
    for copy in copies:
        copy.wait_recv()


def hops(depth, layer):
    far, near = depth // 2, depth - 1 - depth // 2
    return (far, near) if layer % 2 == 0 else (near, far)


def power_kernel(layers, side, depth, q_ref, m_ref, p_ref, g_ref, qall, part, chain, gpart, gcore, a_ref, s1, b_ref, s2, c_ref, s3, d_ref, send, recv):
    me = Place(side, depth)
    wire = Wire(send, recv)
    x, y, c, z = me.x, me.y, me.c, me.z
    rank = g_ref.shape[-1]
    me.barrier()

    qall[:, x, y, c] = q_ref[...]
    first = [
        [wire.put(qall.at[l, x, y, c], qall.at[l, x, y, c], me.along(l, t)) for _, t in me.others(l)]
        for l in range(layers)
    ]
    second = []
    for l in range(layers):
        arrive(first[l])
        block = qall.at[l, :, y, c] if l == 0 else qall.at[l, x, :, c]
        second.append([wire.put(block, block, me.along(1 - l, t)) for _, t in me.others(1 - l)])
    third = []
    for l in range(layers):
        arrive(second[l])
        third.append(wire.put(qall.at[l, :, :, c], qall.at[l, :, :, c], me.at(c=1 - c)))

    right, left = lax.rem(z + 1, depth), lax.rem(z + depth - 1, depth)
    rows = part.shape[2]

    def chain_step(l, way, s):
        count = hops(depth, l)[way]
        ahead = count - s + 1
        dest = lax.rem(z + ahead, depth) if way == 0 else lax.rem(z + depth - ahead, depth)
        src = part.at[l, dest]
        if s > 1:
            src = chain.at[l, way, s - 2]
            src[...] += part[l, dest]
        return wire.put(src, chain.at[l, way, s - 1], me.at(z=right if way == 0 else left))

    pending = {}
    for l in range(layers):
        third[l].wait_recv()
        factor = qall[l].reshape(rank, -1)

        @pl.loop(0, depth // 2)
        def _(i):
            lhs = m_ref[l, pl.ds(pl.multiple_of(i * 2 * rows, 16), 2 * rows), :]
            out = lax.dot_general(lhs, factor, (((1,), (1,)), ((), ())), preferred_element_type=F32)
            part[l, pl.ds(2 * i, 2)] = out.reshape(2, rows, rank)

        for way in (0, 1):
            if hops(depth, l)[way]:
                pending[l, way] = chain_step(l, way, 1)
    for s in range(2, depth // 2 + 1):
        for l in range(layers):
            for way in (0, 1):
                if s <= hops(depth, l)[way]:
                    pending[l, way].wait_recv()
                    pending[l, way] = chain_step(l, way, s)
    for l in range(layers):
        total = part[l, z]
        for way in (0, 1):
            count = hops(depth, l)[way]
            if count:
                pending[l, way].wait_recv()
                total = total + chain[l, way, count - 1]
        p_ref[l] = total
        gram = lax.dot_general(total, total, (((0,), (0,)), ((), ())), precision=HI, preferred_element_type=F32)
        gpart[l] = gram.reshape(gpart.shape[1:])

    wire.put(gpart.at[1 - c], gcore, me.at(c=1 - c)).wait_recv()
    a_ref[...] = gpart[c] + gcore[...]
    copies = [
        [wire.put(a_ref.at[h, t], s1.at[h, o - 1], me.along(h, t)) for o, t in me.others(h)] for h in (0, 1)
    ]
    for h in (0, 1):
        arrive(copies[h])
        total = a_ref[h, me.mine(h)]
        for o in range(side - 1):
            total = total + s1[h, o]
        b_ref[h] = total
        copies[h] = [wire.put(b_ref.at[h, t], s2.at[h, o - 1], me.along(1 - h, t)) for o, t in me.others(1 - h)]
    wide = 2 * rank // depth
    tall = b_ref.shape[2] // 2
    tile = lambda t: (slice(t // (depth // 2) * tall, t // (depth // 2) * tall + tall), slice(t % (depth // 2) * wide, t % (depth // 2) * wide + wide))
    for h in (0, 1):
        arrive(copies[h])
        total = b_ref[h, me.mine(1 - h)]
        for o in range(side - 1):
            total = total + s2[h, o]
        for t in range(depth):
            c_ref[t, h] = total[tile(t)]
    arrive([wire.put(c_ref.at[t], s3.at[o - 1], me.at(z=t)) for o, t in me.others_z()])
    total = c_ref[z]
    for o in range(depth - 1):
        total = total + s3[o]
    d_ref[z] = total
    arrive([wire.put(d_ref.at[z], d_ref.at[z], me.at(z=t)) for _, t in me.others_z()])
    for h in (0, 1):
        i, j = me.mine(h), me.mine(1 - h)
        for t in range(depth):
            g_ref[(c, h, i, j) + tile(t)] = d_ref[t, h]
        copies[h] = [
            wire.put(g_ref.at[c, h, i, j], g_ref.at[c, h, i, j], me.along(1 - h, t)) for _, t in me.others(1 - h)
        ]
    for h in (0, 1):
        arrive(copies[h])
        i = me.mine(h)
        copies[h] = [wire.put(g_ref.at[c, h, i], g_ref.at[c, h, i], me.along(h, t)) for _, t in me.others(h)]
    for h in (0, 1):
        arrive(copies[h])
    wire.put(g_ref.at[c], g_ref.at[c], me.at(c=1 - c)).wait_recv()
    wire.finish()


def power(momentum, factor, side, depth):
    layers, rows, width = momentum.shape
    rank = factor.shape[1] * side * side * CORES
    short = rows // depth
    piece = rank // (2 * side * side)
    tile = (depth, 2, piece // 2, 2 * rank // depth)
    steps = layers * (2 * (side - 1) + 1) + layers * (depth - 1)
    steps += 2 + 8 * (side - 1) + 2 * (depth - 1)
    whole = (2, side, side, piece, rank)
    far = max(1, depth // 2)
    p, g = pl.pallas_call(
        functools.partial(power_kernel, layers, side, depth),
        out_shape=(
            jax.ShapeDtypeStruct((layers, short, rank), F32),
            jax.ShapeDtypeStruct((layers,) + whole, F32),
        ),
        in_specs=[pl.BlockSpec(memory_space=pltpu.VMEM)] * 2,
        out_specs=[pl.BlockSpec(memory_space=pltpu.VMEM)] * 2,
        scratch_shapes=[
            pltpu.VMEM((layers, side, side, CORES, factor.shape[1], width), BF16),
            pltpu.VMEM((layers, depth, short, rank), F32),
            pltpu.VMEM((layers, 2, far, short, rank), F32),
            pltpu.VMEM((layers,) + whole, F32),
            pltpu.VMEM(whole, F32),
            pltpu.VMEM(whole, F32),
            pltpu.VMEM((2, side - 1) + whole[2:], F32),
            pltpu.VMEM((2,) + whole[2:], F32),
            pltpu.VMEM((2, side - 1) + whole[3:], F32),
            pltpu.VMEM(tile, F32),
            pltpu.VMEM((depth - 1,) + tile[1:], F32),
            pltpu.VMEM(tile, F32),
            pltpu.SemaphoreType.DMA((steps,)),
            pltpu.SemaphoreType.DMA((steps,)),
        ],
        compiler_params=pltpu.CompilerParams(collective_id=0, has_side_effects=True, vmem_limit_bytes=VMEM_BYTES),
        name="power_gram",
    )(factor, momentum)
    return p, g.reshape(layers, rank, rank)


def right_kernel(layers, side, depth, o_ref, m_ref, all_ref, pair_ref, new_ref, rt, rc, r1, u, r2, sq, sz, send, recv):
    me = Place(side, depth)
    wire = Wire(send, recv)
    x, y, c, z = me.x, me.y, me.c, me.z
    rank = o_ref.shape[-1]
    me.barrier()

    right, left = lax.rem(z + 1, depth), lax.rem(z + depth - 1, depth)
    all_ref[:, z] = o_ref[...]

    def chain_step(l, way, s):
        src = lax.rem(z + depth - (s - 1), depth) if way == 0 else lax.rem(z + s - 1, depth)
        return wire.put(all_ref.at[l, src], all_ref.at[l, src], me.at(z=right if way == 0 else left))

    for l in range(layers):
        pending = {}
        for s in range(1, depth // 2 + 1):
            for way in (0, 1):
                if s <= hops(depth, l)[way]:
                    if s > 1:
                        pending[way].wait_recv()
                    pending[way] = chain_step(l, way, s)
        for way in pending:
            pending[way].wait_recv()
    core = []
    for l in range(layers):
        ortho = all_ref[l].reshape(-1, rank)
        width = m_ref.shape[-1]
        for k in range(width // 256):
            cols = slice(256 * k, 256 * k + 256)
            out = lax.dot_general(ortho, m_ref[l, :, cols], (((0,), (0,)), ((), ())), preferred_element_type=F32)
            rt[l, :, :, :, :, cols] = out.reshape(rt.shape[1:5] + (256,))
        core.append(wire.put(rt.at[l, :, :, 1 - c], rc.at[l], me.at(c=1 - c)))

    copies = []
    for l in range(layers):
        core[l].wait_recv()
        rt[l, :, :, c] += rc[l]
        pick = lambda t: rt.at[l, t, :, c] if l == 0 else rt.at[l, :, t, c]
        copies.append([wire.put(pick(t), r1.at[l, o - 1], me.along(l, t)) for o, t in me.others(l)])
    for l in range(layers):
        arrive(copies[l])
        total = rt[l, x, :, c] if l == 0 else rt[l, :, y, c]
        for o in range(side - 1):
            total = total + r1[l, o]
        u[l] = total
        copies[l] = [wire.put(u.at[l, t], r2.at[l, o - 1], me.along(1 - l, t)) for o, t in me.others(1 - l)]
    sums = []
    for l in range(layers):
        arrive(copies[l])
        total = u[l, me.mine(1 - l)]
        for o in range(side - 1):
            total = total + r2[l, o]
        sums.append(total)
        sq[l] = jnp.broadcast_to(jnp.sum(total * total, axis=1, keepdims=True), sq.shape[1:])
    arrive([wire.put(sq, sz.at[o - 1], me.at(z=t)) for o, t in me.others_z()])
    norm = sq[...]
    for o in range(depth - 1):
        norm = norm + sz[o]
    for l in range(layers):
        normed = (sums[l] * lax.rsqrt(norm[l, :, :1] + 1e-06)).astype(BF16)
        new_ref[l] = normed
        pair_ref[l, 0, x, y, c] = sums[l].astype(BF16)
        pair_ref[l, 1, x, y, c] = normed
        block = pair_ref.at[l, :, x, y, c]
        copies[l] = [wire.put(block, block, me.along(l, t)) for _, t in me.others(l)]
    for l in range(layers):
        arrive(copies[l])
        block = pair_ref.at[l, :, :, y, c] if l == 0 else pair_ref.at[l, :, x, :, c]
        copies[l] = [wire.put(block, block, me.along(1 - l, t)) for _, t in me.others(1 - l)]
    last = []
    for l in range(layers):
        arrive(copies[l])
        block = pair_ref.at[l, :, :, :, c]
        last.append(wire.put(block, block, me.at(c=1 - c)))
    arrive(last)
    wire.finish()


def right_products(ortho, momentum, side, depth):
    layers, rows, width = momentum.shape
    rank = ortho.shape[-1]
    per = rank // (side * side * CORES)
    steps = layers * (depth - 1) + 2 * layers + (depth - 1) + layers * 4 * (side - 1)
    grid = (side, side, CORES, per, width)
    whole, pair, new = pl.pallas_call(
        functools.partial(right_kernel, layers, side, depth),
        out_shape=(
            jax.ShapeDtypeStruct((layers, depth) + ortho.shape[1:], BF16),
            jax.ShapeDtypeStruct((layers, 2) + grid, BF16),
            jax.ShapeDtypeStruct((layers, per, width), BF16),
        ),
        in_specs=[pl.BlockSpec(memory_space=pltpu.VMEM)] * 2,
        out_specs=[pl.BlockSpec(memory_space=pltpu.VMEM)] * 3,
        scratch_shapes=[
            pltpu.VMEM((layers,) + grid, F32),
            pltpu.VMEM((layers, side, side, per, width), F32),
            pltpu.VMEM((layers, side - 1, side, per, width), F32),
            pltpu.VMEM((layers, side, per, width), F32),
            pltpu.VMEM((layers, side - 1, per, width), F32),
            pltpu.VMEM((layers, per, 128), F32),
            pltpu.VMEM((depth - 1, layers, per, 128), F32),
            pltpu.SemaphoreType.DMA((steps,)),
            pltpu.SemaphoreType.DMA((steps,)),
        ],
        compiler_params=pltpu.CompilerParams(collective_id=1, has_side_effects=True, vmem_limit_bytes=VMEM_BYTES),
        name="right_products",
    )(ortho, momentum)
    return whole.reshape(layers, rows, rank), pair.reshape(layers, 2, rank, width), new


def leaf_inverse(x):
    groups = NB // 8
    rows = [x[8 * g : 8 * g + 8, :] for g in range(groups)]
    lane = lax.broadcasted_iota(jnp.int32, (8, NB), 1)
    sub = lax.broadcasted_iota(jnp.int32, (8, NB), 0)
    splat = lambda v, p: jnp.broadcast_to(v[p : p + 1, :], (8, NB))
    out = []
    for g in range(groups):
        base = 8 * g
        inside = (lane >= base) & (lane < base + 8)
        cur = rows[g]
        cols = [jnp.broadcast_to(cur[:, base + q : base + q + 1], (8, NB)) for q in range(8)]
        fwd = jnp.where(inside, jnp.where(lane == sub + base, 1.0, 0.0), cur)
        full = fwd
        pivot = None
        for p in range(8):
            d = splat(cols[p], p)
            m = cols[p] * (1.0 / d)
            mf = jnp.where(sub > p, m, 0.0)
            mj = jnp.where(sub == p, 0.0, m)
            pivot = d if p == 0 else jnp.where(sub == p, d, pivot)
            if p < 7:
                fwd = fwd - mf * splat(fwd, p)
            full = full - mj * splat(full, p)
            for q in range(p + 1, 8):
                cols[q] = cols[q] - mj * splat(cols[q], p)
        out.append(jnp.where(lane < base + 8, fwd * lax.rsqrt(pivot), 0.0))
        if g + 1 < groups:
            full = full / pivot
            parts = [splat(full, q) for q in range(8)]
            for i in range(g + 1, groups):
                r = rows[i]
                acc = jnp.where(inside, 0.0, r)
                for q in range(8):
                    acc = acc - jnp.broadcast_to(r[:, base + q : base + q + 1], (8, NB)) * parts[q]
                rows[i] = acc
    return jnp.concatenate(out, axis=0)

def chol_kernel(layers, n, gram_ref, proj_ref, out_ref, x_ref):
    blocks = n // NB
    x_ref[...] = gram_ref[...]
    colid = lax.broadcasted_iota(jnp.int32, (NB, n), 1) // NB
    ident = (lax.broadcasted_iota(jnp.int32, (NB, n), 1) % NB == lax.broadcasted_iota(jnp.int32, (NB, n), 0)).astype(F32)
    def step(k, carry):
        w = [leaf_inverse(x_ref[l, pl.ds(k * NB, NB), pl.ds(k * NB, NB)]) for l in range(layers)]
        return carry
    for k in range(blocks):
        sl = slice(k * NB, k * NB + NB)
        ws = [leaf_inverse(x_ref[l, sl, sl]) for l in range(layers)]
        for l in range(layers):
            row = jnp.where(colid == k, ident, x_ref[l, sl, :])
            y = jnp.dot(ws[l], row, precision=HI, preferred_element_type=F32)
            x_ref[l, sl, :] = jnp.where(colid <= k, y, 0.0)
            if k + 1 < blocks:
                tail = slice(k * NB + NB, n)
                upd = lax.dot_general(y[:, k * NB + NB :], y, (((0,), (0,)), ((), ())), precision=HI, preferred_element_type=F32)
                keep = x_ref[l, tail, :]
                cid = lax.broadcasted_iota(jnp.int32, keep.shape, 1) // NB
                x_ref[l, tail, :] = jnp.where(cid == k, 0.0, keep) - upd
    for l in range(layers):
        out_ref[l] = lax.dot_general(proj_ref[l], x_ref[l], (((1,), (1,)), ((), ())), precision=HI, preferred_element_type=F32).astype(out_ref.dtype)

def chol_ortho(gram, proj):
    layers, n, _ = gram.shape
    return pl.pallas_call(
        functools.partial(chol_kernel, layers, n),
        out_shape=jax.ShapeDtypeStruct(proj.shape, BF16),
        in_specs=[pl.BlockSpec(memory_space=pltpu.VMEM)] * 2,
        out_specs=pl.BlockSpec(memory_space=pltpu.VMEM),
        scratch_shapes=[pltpu.VMEM((layers, n, n), F32)],
        compiler_params=pltpu.CompilerParams(vmem_limit_bytes=48 * 2**20),
    )(gram, proj)


def solution(mesh):
    side = math.isqrt(mesh.shape["fsdp"] // CORES)
    depth = mesh.shape["tp"]

    def local(momentum, right_factor):
        rank = right_factor.shape[1] * side * side * CORES
        total_rows, total_cols = momentum.shape[1] * side * side * CORES, momentum.shape[2] * depth
        scale = math.sqrt(total_rows * total_cols / rank)
        project, gram = power(momentum, right_factor, side, depth)
        ortho_part = chol_ortho(gram, project)
        ortho, pair, new_factor = right_products(ortho_part, momentum, side, depth)
        feedback = jnp.einsum("lrk,lkd->lrd", ortho, pair[:, 0], preferred_element_type=F32)
        direction = jnp.einsum("lrk,lkd->lrd", ortho, pair[:, 1], preferred_element_type=F32)
        new_momentum = (momentum.astype(F32) - 0.05 * feedback).astype(BF16)
        return new_momentum, (scale * direction).astype(BF16), new_factor

    spec = P(None, "fsdp", "tp")
    return jax.shard_map(local, mesh=mesh, in_specs=(spec, spec), out_specs=(spec, spec, spec), check_vma=False)
```

```python
import functools
import math

import jax
import jax.numpy as jnp
from jax import lax
from jax.experimental import pallas as pl
from jax.experimental.pallas import tpu as pltpu
from jax.sharding import PartitionSpec as P

MESH = pl.DeviceIdType.MESH
HI = lax.Precision.HIGHEST
CORES = 2
NB = 128
VMEM_BYTES = 36 * 2**20
F32 = jnp.float32
BF16 = jnp.bfloat16


class Place:
    def __init__(self, side, depth):
        f, self.z = lax.axis_index("fsdp"), lax.axis_index("tp")
        self.side, self.depth = side, depth
        self.x, self.y, self.c = f // (side * CORES), (f // CORES) % side, f % CORES

    def at(self, x=None, y=None, c=None, z=None):
        x = self.x if x is None else x
        y = self.y if y is None else y
        c = self.c if c is None else c
        z = self.z if z is None else z
        return ((x * self.side + y) * CORES + c, z)

    def along(self, axis, t):
        return self.at(x=t) if axis == 0 else self.at(y=t)

    def mine(self, axis):
        return self.x if axis == 0 else self.y

    def others(self, axis):
        return [(o, lax.rem(self.mine(axis) + o, self.side)) for o in range(1, self.side)]

    def others_z(self):
        return [(o, lax.rem(self.z + o, self.depth)) for o in range(1, self.depth)]

    def barrier(self):
        sem = pltpu.get_barrier_semaphore()
        devices = [self.at(c=1 - self.c)]
        devices += [self.along(a, t) for a in (0, 1) for _, t in self.others(a)]
        devices += [self.at(z=t) for _, t in self.others_z()]
        for device in devices:
            pl.semaphore_signal(sem, inc=1, device_id=device, device_id_type=MESH)
        pl.semaphore_wait(sem, len(devices))


class Wire:
    def __init__(self, send, recv):
        self.send, self.recv, self.used, self.copies = send, recv, 0, []

    def put(self, src, dst, device):
        n = self.used
        self.used += 1
        copy = pltpu.make_async_remote_copy(
            src_ref=src,
            dst_ref=dst,
            send_sem=self.send.at[n],
            recv_sem=self.recv.at[n],
            device_id=device,
            device_id_type=MESH,
        )
        copy.start()
        self.copies.append(copy)
        return copy

    def finish(self):
        for copy in self.copies:
            copy.wait_send()


def halves(ref):
    wide = ref.shape[-1] // 2
    lead = (slice(None),) * (len(ref.shape) - 1)
    return ref.at[lead + (slice(0, wide),)], ref.at[lead + (slice(wide, 2 * wide),)]


def gather_ring(me, wire, axis, pick):
    t, n = me.mine(axis), me.side
    after, before = lax.rem(t + 1, n), lax.rem(t + n - 1, n)
    if n == 2:
        copies = [wire.put(pick(t), pick(t), me.along(axis, after))]
    else:
        up = wire.put(pick(t), pick(t), me.along(axis, after))
        down = wire.put(pick(t), pick(t), me.along(axis, before))
        yield
        up.wait_recv()
        block = halves(pick(before))[0]
        copies = [wire.put(block, block, me.along(axis, after))]
        down.wait_recv()
        block = halves(pick(after))[1]
        copies.append(wire.put(block, block, me.along(axis, before)))
    yield
    arrive(copies)


def reduce_ring(me, wire, axis, pick, far, near, out):
    t, n = me.mine(axis), me.side
    after, before = lax.rem(t + 1, n), lax.rem(t + n - 1, n)
    if n == 2:
        copies = [wire.put(pick(after), near.at[0], me.along(axis, after))]
    else:
        up, down = me.along(axis, after), me.along(axis, before)
        cross = halves(pick(lax.rem(t + 2, n)))
        to_up, to_down = halves(pick(after)), halves(pick(before))
        at_up, at_down = halves(near.at[0]), halves(near.at[1])
        first = [wire.put(cross[0], far.at[0], up), wire.put(cross[1], far.at[1], down)]
        copies = [wire.put(to_up[1], at_up[1], up), wire.put(to_down[0], at_down[0], down)]
        yield
        first[0].wait_recv()
        to_up[0][...] += far[0]
        copies.append(wire.put(to_up[0], at_up[0], up))
        first[1].wait_recv()
        to_down[1][...] += far[1]
        copies.append(wire.put(to_down[1], at_down[1], down))
    yield
    arrive(copies)
    out[...] = pick(t)[...] + near[0] if n == 2 else pick(t)[...] + near[0] + near[1]


def gather_direct(me, wire, axis, pick):
    mine = pick(me.mine(axis))
    copies = [wire.put(mine, mine, me.along(axis, t)) for _, t in me.others(axis)]
    yield
    arrive(copies)


def reduce_direct(me, wire, axis, pick, near, out):
    copies = [wire.put(pick(t), near.at[o - 1], me.along(axis, t)) for o, t in me.others(axis)]
    yield
    arrive(copies)
    total = pick(me.mine(axis))[...]
    for o in range(me.side - 1):
        total = total + near[o]
    out[...] = total


def together(*parts):
    parts = list(parts)
    while parts:
        for part in list(parts):
            if next(part, parts) is parts:
                parts.remove(part)


def arrive(copies):
    for copy in copies:
        copy.wait_recv()


def hops(depth, layer):
    far, near = depth // 2, depth - 1 - depth // 2
    return (far, near) if layer % 2 == 0 else (near, far)


def staged(parts):
    while parts:
        for part in list(parts):
            if next(part, parts) is parts:
                parts.remove(part)
        if parts:
            yield


def place_block(ref, n, block):
    piece = ref.shape[-2]
    flat, side = n * NB, ref.shape[1]
    done = 0
    while done < NB:
        index, offset = (flat + done) // piece, (flat + done) % piece
        rows = min(piece - offset, NB - done)
        ref[index // (side * side), index // side % side, index % side, offset : offset + rows] = block[done : done + rows]
        done += rows


def power_kernel(layers, side, depth, q_ref, m_hbm, p_ref, g_ref, m_ref, qall, part, chain, pcore, a_ref, near1, b_ref, near2, t_ref, s3, send, recv, load):
    me = Place(side, depth)
    wire = Wire(send, recv)
    x, y, c, z = me.x, me.y, me.c, me.z
    rank = p_ref.shape[-1]
    loads = [pltpu.make_async_copy(m_hbm.at[l], m_ref.at[l], load.at[l]) for l in range(layers)]
    for copy in loads:
        copy.start()
    qall[:, x, y, c] = q_ref[...]
    me.barrier()

    def factor_rows(l):
        yield from gather_direct(me, wire, l, lambda t: qall.at[l, t, y, c] if l == 0 else qall.at[l, x, t, c])
        yield from gather_direct(me, wire, 1 - l, lambda t: qall.at[l, :, t, c] if l == 0 else qall.at[l, t, :, c])
        crossing.append(wire.put(qall.at[l, :, :, c], qall.at[l, :, :, c], me.at(c=1 - c)))

    crossing = []
    together(*[factor_rows(l) for l in range(layers)])

    right, left = lax.rem(z + 1, depth), lax.rem(z + depth - 1, depth)
    rows = part.shape[2]

    def chain_step(l, way, s):
        count = hops(depth, l)[way]
        ahead = count - s + 1
        dest = lax.rem(z + ahead, depth) if way == 0 else lax.rem(z + depth - ahead, depth)
        src = part.at[l, dest]
        if s > 1:
            src = chain.at[l, way, s - 2]
            src[...] += part[l, dest]
        return wire.put(src, chain.at[l, way, s - 1], me.at(z=right if way == 0 else left))

    pending = {}
    for l in range(layers):
        crossing[l].wait_recv()
        loads[l].wait()
        factor = qall[l].reshape(rank, -1)

        @pl.loop(0, depth // 2)
        def _(i):
            lhs = m_ref[l, pl.ds(pl.multiple_of(i * 2 * rows, 16), 2 * rows), :]
            out = lax.dot_general(lhs, factor, (((1,), (1,)), ((), ())), preferred_element_type=F32)
            part[l, pl.ds(2 * i, 2)] = out.reshape(2, rows, rank)

        for way in (0, 1):
            if hops(depth, l)[way]:
                pending[l, way] = chain_step(l, way, 1)
    for s in range(2, depth // 2 + 1):
        for l in range(layers):
            for way in (0, 1):
                if s <= hops(depth, l)[way]:
                    pending[l, way].wait_recv()
                    pending[l, way] = chain_step(l, way, s)
    for l in range(layers):
        total = part[l, z]
        for way in (0, 1):
            count = hops(depth, l)[way]
            if count:
                pending[l, way].wait_recv()
                total = total + chain[l, way, count - 1]
        p_ref[l, z] = total

    def gather_project(l):
        pending = {}
        for s in range(1, depth // 2 + 1):
            for way in (0, 1):
                if s <= hops(depth, l)[way]:
                    if s > 1:
                        pending[way].wait_recv()
                    src = lax.rem(z + depth - (s - 1), depth) if way == 0 else lax.rem(z + s - 1, depth)
                    block = p_ref.at[l, src]
                    pending[way] = wire.put(block, block, me.at(z=right if way == 0 else left))
            yield
        arrive(list(pending.values()))

    def sum_gram():
        swap = wire.put(p_ref.at[1 - c, z], pcore, me.at(c=1 - c))
        yield
        swap.wait_recv()
        both = jnp.concatenate([p_ref[c, z], pcore[...]], axis=0)
        blocks = rank // NB
        n = 0
        for i in range(blocks):
            gram = lax.dot_general(both[:, i * NB : i * NB + NB], both[:, i * NB :], (((0,), (0,)), ((), ())), precision=HI, preferred_element_type=F32)
            for j in range(blocks - i):
                place_block(a_ref, n, gram[:, j * NB : j * NB + NB])
                n += 1
        planes = [sum_plane(0), sum_plane(1)]
        yield from staged(planes)
        copies = [wire.put(t_ref, s3.at[o - 1], me.at(z=t)) for o, t in me.others_z()]
        yield
        arrive(copies)
        total = t_ref[...]
        for o in range(depth - 1):
            total = total + s3[o]
        for h in (0, 1):
            g_ref[h, me.mine(h), me.mine(1 - h)] = total[h]
        yield from staged([spread_plane(0), spread_plane(1)])

    def sum_plane(h):
        yield from reduce_direct(me, wire, h, lambda t: a_ref.at[h, t], near1.at[h], b_ref.at[h])
        yield from reduce_direct(me, wire, 1 - h, lambda t: b_ref.at[h, t], near2.at[h], t_ref.at[h])

    def spread_plane(h):
        i = me.mine(h)
        yield from gather_direct(me, wire, 1 - h, lambda t: g_ref.at[h, i, t])
        yield from gather_direct(me, wire, h, lambda t: g_ref.at[h, t])

    together(sum_gram(), *[gather_project(l) for l in range(layers)])
    wire.finish()


def power(momentum, factor, side, depth):
    layers, rows, width = momentum.shape
    rank = factor.shape[1] * side * side * CORES
    short = rows // depth
    blocks = rank // NB
    piece = blocks * (blocks + 1) // 2 * NB // (2 * side * side)
    whole = (2, side, side, piece, NB)
    p, g = pl.pallas_call(
        functools.partial(power_kernel, layers, side, depth),
        out_shape=(
            jax.ShapeDtypeStruct((layers, depth, short, rank), F32),
            jax.ShapeDtypeStruct(whole, F32),
        ),
        in_specs=[pl.BlockSpec(memory_space=pltpu.VMEM), pl.BlockSpec(memory_space=pl.ANY)],
        out_specs=[pl.BlockSpec(memory_space=pltpu.VMEM)] * 2,
        scratch_shapes=[
            pltpu.VMEM(momentum.shape, BF16),
            pltpu.VMEM((layers, side, side, CORES, factor.shape[1], width), BF16),
            pltpu.VMEM((layers, depth, short, rank), F32),
            pltpu.VMEM((layers, 2, max(1, depth // 2), short, rank), F32),
            pltpu.VMEM((short, rank), F32),
            pltpu.VMEM(whole, F32),
            pltpu.VMEM((2, side - 1) + whole[2:], F32),
            pltpu.VMEM((2,) + whole[2:], F32),
            pltpu.VMEM((2, side - 1) + whole[3:], F32),
            pltpu.VMEM((2,) + whole[3:], F32),
            pltpu.VMEM((depth - 1, 2) + whole[3:], F32),
            pltpu.SemaphoreType.DMA((100,)),
            pltpu.SemaphoreType.DMA((100,)),
            pltpu.SemaphoreType.DMA((layers,)),
        ],
        compiler_params=pltpu.CompilerParams(collective_id=0, has_side_effects=True, vmem_limit_bytes=VMEM_BYTES),
        name="power_gram",
    )(factor, momentum)
    return p, g.reshape(-1, NB, NB)


def right_kernel(layers, side, depth, w_ref, p_hbm, m_hbm, all_ref, rb_ref, s_ref, new_ref, m_ref, p_ref, wall, rt, rc, far1, near1, u, far2, near2, tot, sq, sz, send, recv, load):
    me = Place(side, depth)
    wire = Wire(send, recv)
    x, y, c, z = me.x, me.y, me.c, me.z
    rank = w_ref.shape[-1]
    loads = [pltpu.make_async_copy(m_hbm.at[l], m_ref.at[l], load.at[l]) for l in range(layers)]
    ploads = [pltpu.make_async_copy(p_hbm.at[l], p_ref.at[l], load.at[layers + l]) for l in range(layers)]
    for copy in ploads + loads:
        copy.start()
    wall[c] = w_ref[...]
    me.barrier()

    wire.put(wall.at[c], wall.at[c], me.at(c=1 - c)).wait_recv()
    core = []
    for l in range(layers):
        ploads[l].wait()

        @pl.loop(0, depth // 2)
        def _(i):
            lhs = p_ref[l, pl.ds(2 * i, 2)].reshape(-1, rank)
            out = lax.dot_general(lhs, wall[l], (((1,), (1,)), ((), ())), precision=HI, preferred_element_type=F32)
            all_ref[l, pl.ds(2 * i, 2)] = out.astype(BF16).reshape(2, -1, rank)

        loads[l].wait()
        ortho = all_ref[l].reshape(-1, rank)
        width = m_ref.shape[-1]
        for k in range(width // 256):
            cols = slice(256 * k, 256 * k + 256)
            out = lax.dot_general(ortho, m_ref[l, :, cols], (((0,), (0,)), ((), ())), preferred_element_type=F32)
            rt[l, :, :, :, :, cols] = out.reshape(rt.shape[1:5] + (256,))
        core.append(wire.put(rt.at[l, :, :, 1 - c], rc.at[l], me.at(c=1 - c)))

    def sum_rows(l):
        core[l].wait_recv()
        rc[l] += rt[l, :, :, c]
        pick = lambda t: rc.at[l, t] if l == 0 else rc.at[l, :, t]
        yield from reduce_ring(me, wire, l, pick, far1.at[l], near1.at[l], u.at[l])
        yield from reduce_ring(me, wire, 1 - l, lambda t: u.at[l, t], far2.at[l], near2.at[l], tot.at[l])

    together(*[sum_rows(l) for l in range(layers)])

    def gather_rows(l):
        rb_ref[l, x, y, c] = tot[l].astype(BF16)
        yield from gather_ring(me, wire, l, lambda t: rb_ref.at[l, t, y, c] if l == 0 else rb_ref.at[l, x, t, c])
        yield from gather_ring(me, wire, 1 - l, lambda t: rb_ref.at[l, :, t, c] if l == 0 else rb_ref.at[l, t, :, c])
        cross = wire.put(rb_ref.at[l, :, :, c], rb_ref.at[l, :, :, c], me.at(c=1 - c))
        yield
        yield
        cross.wait_recv()

    def gather_norms():
        for l in range(layers):
            sq[l] = jnp.broadcast_to(jnp.sum(tot[l] * tot[l], axis=1, keepdims=True), sq.shape[1:])
        copies = [wire.put(sq, sz.at[o - 1], me.at(z=t)) for o, t in me.others_z()]
        yield
        arrive(copies)
        norm = sq[...]
        for o in range(depth - 1):
            norm = norm + sz[o]
        factor = lax.rsqrt(norm + 1e-06)
        for l in range(layers):
            s_ref[l, x, y, c] = factor[l]
            new_ref[l] = (tot[l] * factor[l, :, :1]).astype(BF16)
        mine = s_ref.at[:, x, y, c]
        copies = [wire.put(mine, mine, me.along(0, t)) for _, t in me.others(0)]
        yield
        arrive(copies)
        mine = s_ref.at[:, :, y, c]
        copies = [wire.put(mine, mine, me.along(1, t)) for _, t in me.others(1)]
        yield
        arrive(copies)
        copies = [wire.put(s_ref.at[:, :, :, c], s_ref.at[:, :, :, c], me.at(c=1 - c))]
        yield
        arrive(copies)

    together(*[gather_rows(l) for l in range(layers)], gather_norms())
    wire.finish()


def right_products(inverse, project, momentum, side, depth):
    layers, rows, width = momentum.shape
    rank = project.shape[-1]
    per = rank // (side * side * CORES)
    grid = (side, side, CORES, per)
    whole, rb, s, new = pl.pallas_call(
        functools.partial(right_kernel, layers, side, depth),
        out_shape=(
            jax.ShapeDtypeStruct(project.shape, BF16),
            jax.ShapeDtypeStruct((layers,) + grid + (width,), BF16),
            jax.ShapeDtypeStruct((layers,) + grid + (128,), F32),
            jax.ShapeDtypeStruct((layers, per, width), BF16),
        ),
        in_specs=[pl.BlockSpec(memory_space=pltpu.VMEM)] + [pl.BlockSpec(memory_space=pl.ANY)] * 2,
        out_specs=[pl.BlockSpec(memory_space=pltpu.VMEM)] * 4,
        scratch_shapes=[
            pltpu.VMEM(momentum.shape, BF16),
            pltpu.VMEM(project.shape, F32),
            pltpu.VMEM((layers, rank, rank), F32),
            pltpu.VMEM((layers,) + grid + (width,), F32),
            pltpu.VMEM((layers, side, side, per, width), F32),
            pltpu.VMEM((layers, 2, side, per, width // 2), F32),
            pltpu.VMEM((layers, 2, side, per, width), F32),
            pltpu.VMEM((layers, side, per, width), F32),
            pltpu.VMEM((layers, 2, per, width // 2), F32),
            pltpu.VMEM((layers, 2, per, width), F32),
            pltpu.VMEM((layers, per, width), F32),
            pltpu.VMEM((layers, per, 128), F32),
            pltpu.VMEM((depth - 1, layers, per, 128), F32),
            pltpu.SemaphoreType.DMA((100,)),
            pltpu.SemaphoreType.DMA((100,)),
            pltpu.SemaphoreType.DMA((2 * layers,)),
        ],
        compiler_params=pltpu.CompilerParams(collective_id=1, has_side_effects=True, vmem_limit_bytes=VMEM_BYTES),
        name="right_products",
    )(inverse, project, momentum)
    return whole.reshape(layers, rows, rank), rb.reshape(layers, rank, width), s.reshape(layers, rank, 128), new


def final_kernel(scale, o_ref, m_ref, rb_ref, s_ref, mom_ref, up_ref):
    ortho, rb = o_ref[0], rb_ref[0]
    feedback = jnp.dot(ortho, rb, preferred_element_type=F32)
    mom_ref[0] = (m_ref[0].astype(F32) - 0.05 * feedback).astype(BF16)
    normed = (rb.astype(F32) * s_ref[0, :, :1]).astype(BF16)
    up_ref[0] = (scale * jnp.dot(ortho, normed, preferred_element_type=F32)).astype(BF16)


def final_products(ortho, momentum, rb, s, scale):
    layers, rows, rank = ortho.shape
    width = momentum.shape[-1]
    block = min(width, 256)
    cols = lambda n: pl.BlockSpec((1, n, block), lambda l, i: (l, 0, i))
    full = lambda n, w: pl.BlockSpec((1, n, w), lambda l, i: (l, 0, 0))
    return pl.pallas_call(
        functools.partial(final_kernel, scale),
        grid=(layers, width // block),
        out_shape=[jax.ShapeDtypeStruct(momentum.shape, BF16)] * 2,
        in_specs=[full(rows, rank), cols(rows), cols(rank), full(rank, 128)],
        out_specs=[cols(rows)] * 2,
        compiler_params=pltpu.CompilerParams(vmem_limit_bytes=VMEM_BYTES),
        name="final_products",
    )(ortho, momentum, rb, s)


def leaf_inverse(x):
    groups = NB // 8
    rows = [x[8 * g : 8 * g + 8, :] for g in range(groups)]
    lane = lax.broadcasted_iota(jnp.int32, (8, NB), 1)
    sub = lax.broadcasted_iota(jnp.int32, (8, NB), 0)
    splat = lambda v, p: jnp.broadcast_to(v[p : p + 1, :], (8, NB))
    out = []
    for g in range(groups):
        base = 8 * g
        inside = (lane >= base) & (lane < base + 8)
        cur = rows[g]
        cols = [jnp.broadcast_to(cur[:, base + q : base + q + 1], (8, NB)) for q in range(8)]
        fwd = jnp.where(inside, jnp.where(lane == sub + base, 1.0, 0.0), cur)
        full = fwd
        pivot = None
        for p in range(8):
            d = splat(cols[p], p)
            inv = pl.reciprocal(d, approx=True)
            inv = inv * (2.0 - d * inv)
            m = cols[p] * inv
            mf = jnp.where(sub > p, m, 0.0)
            mj = jnp.where(sub == p, 0.0, m)
            pivot = d if p == 0 else jnp.where(sub == p, d, pivot)
            ipivot = inv if p == 0 else jnp.where(sub == p, inv, ipivot)
            if p < 7:
                fwd = fwd - mf * splat(fwd, p)
            full = full - mj * splat(full, p)
            for q in range(p + 1, 8):
                cols[q] = cols[q] - mj * splat(cols[q], p)
        out.append(jnp.where(lane < base + 8, fwd * lax.rsqrt(pivot), 0.0))
        if g + 1 < groups:
            full = full * ipivot
            parts = [splat(full, q) for q in range(8)]
            for i in range(g + 1, groups):
                r = rows[i]
                acc = jnp.where(inside, 0.0, r)
                for q in range(8):
                    acc = acc - jnp.broadcast_to(r[:, base + q : base + q + 1], (8, NB)) * parts[q]
                rows[i] = acc
    return jnp.concatenate(out, axis=0)

def chol_kernel(n, gram_ref, x_ref):
    blocks = n // NB
    x_ref[...] = jnp.zeros_like(x_ref)
    b = 0
    for i in range(blocks):
        for j in range(i, blocks):
            x_ref[i * NB : i * NB + NB, j * NB : j * NB + NB] = gram_ref[b]
            b += 1
    colid = lax.broadcasted_iota(jnp.int32, (NB, n), 1) // NB
    ident = (lax.broadcasted_iota(jnp.int32, (NB, n), 1) % NB == lax.broadcasted_iota(jnp.int32, (NB, n), 0)).astype(F32)
    for k in range(blocks):
        sl = slice(k * NB, k * NB + NB)
        w = leaf_inverse(x_ref[sl, sl])
        row = jnp.where(colid == k, ident, x_ref[sl, :])
        out = jnp.dot(w, row, precision=HI, preferred_element_type=F32)
        x_ref[sl, :] = jnp.where(colid <= k, out, 0.0)
        if k + 1 < blocks:
            tail = slice(k * NB + NB, n)
            upd = lax.dot_general(out[:, k * NB + NB :], out, (((0,), (0,)), ((), ())), precision=HI, preferred_element_type=F32)
            keep = x_ref[tail, :]
            cid = lax.broadcasted_iota(jnp.int32, keep.shape, 1) // NB
            x_ref[tail, :] = jnp.where(cid == k, 0.0, keep) - upd


def chol_inverse(gram):
    n = NB * (math.isqrt(8 * gram.shape[0] + 1) // 2)
    return pl.pallas_call(
        functools.partial(chol_kernel, n),
        out_shape=jax.ShapeDtypeStruct((n, n), F32),
        in_specs=[pl.BlockSpec(memory_space=pltpu.VMEM)],
        out_specs=pl.BlockSpec(memory_space=pltpu.VMEM),
        compiler_params=pltpu.CompilerParams(vmem_limit_bytes=VMEM_BYTES),
        name="chol_inverse",
    )(gram)


def solution(mesh):
    side = math.isqrt(mesh.shape["fsdp"] // CORES)
    depth = mesh.shape["tp"]

    def local(momentum, right_factor):
        rank = right_factor.shape[1] * side * side * CORES
        total_rows, total_cols = momentum.shape[1] * side * side * CORES, momentum.shape[2] * depth
        scale = math.sqrt(total_rows * total_cols / rank)
        project, gram = power(momentum, right_factor, side, depth)
        inverse = chol_inverse(gram)
        ortho, rb, s, new_factor = right_products(inverse, project, momentum, side, depth)
        new_momentum, update = final_products(ortho, momentum, rb, s, scale)
        return new_momentum, update, new_factor

    spec = P(None, "fsdp", "tp")
    return jax.shard_map(local, mesh=mesh, in_specs=(spec, spec), out_specs=(spec, spec, spec), check_vma=False)
```

```python
import functools
import math

import jax
import jax.numpy as jnp
from jax import lax
from jax.experimental import pallas as pl
from jax.experimental.pallas import tpu as pltpu
from jax.sharding import PartitionSpec as P

MESH = pl.DeviceIdType.MESH
HI = lax.Precision.HIGHEST
CORES = 2
NB = 128
VMEM_BYTES = 48 * 2**20
F32 = jnp.float32
BF16 = jnp.bfloat16


class Place:
    def __init__(self, side, depth):
        f, self.z = lax.axis_index("fsdp"), lax.axis_index("tp")
        self.side, self.depth = side, depth
        self.x, self.y, self.c = f // (side * CORES), (f // CORES) % side, f % CORES

    def at(self, x=None, y=None, c=None, z=None):
        x = self.x if x is None else x
        y = self.y if y is None else y
        c = self.c if c is None else c
        z = self.z if z is None else z
        return ((x * self.side + y) * CORES + c, z)

    def along(self, axis, t):
        return self.at(x=t) if axis == 0 else self.at(y=t)

    def mine(self, axis):
        return self.x if axis == 0 else self.y

    def others(self, axis):
        return [(o, lax.rem(self.mine(axis) + o, self.side)) for o in range(1, self.side)]

    def others_z(self):
        return [(o, lax.rem(self.z + o, self.depth)) for o in range(1, self.depth)]

    def barrier(self):
        sem = pltpu.get_barrier_semaphore()
        devices = [self.at(c=1 - self.c)]
        devices += [self.along(a, t) for a in (0, 1) for _, t in self.others(a)]
        devices += [self.at(z=t) for _, t in self.others_z()]
        for device in devices:
            pl.semaphore_signal(sem, inc=1, device_id=device, device_id_type=MESH)
        pl.semaphore_wait(sem, len(devices))


class Wire:
    def __init__(self, send, recv):
        self.send, self.recv, self.used, self.copies = send, recv, 0, []

    def put(self, src, dst, device):
        n = self.used
        self.used += 1
        copy = pltpu.make_async_remote_copy(
            src_ref=src,
            dst_ref=dst,
            send_sem=self.send.at[n],
            recv_sem=self.recv.at[n],
            device_id=device,
            device_id_type=MESH,
        )
        copy.start()
        self.copies.append(copy)
        return copy

    def finish(self):
        for copy in self.copies:
            copy.wait_send()


def halves(ref):
    wide = ref.shape[-1] // 2
    lead = (slice(None),) * (len(ref.shape) - 1)
    return ref.at[lead + (slice(0, wide),)], ref.at[lead + (slice(wide, 2 * wide),)]


def gather_ring(me, wire, axis, pick):
    t, n = me.mine(axis), me.side
    after, before = lax.rem(t + 1, n), lax.rem(t + n - 1, n)
    if n == 2:
        copies = [wire.put(pick(t), pick(t), me.along(axis, after))]
    else:
        up = wire.put(pick(t), pick(t), me.along(axis, after))
        down = wire.put(pick(t), pick(t), me.along(axis, before))
        yield
        up.wait_recv()
        block = halves(pick(before))[0]
        copies = [wire.put(block, block, me.along(axis, after))]
        down.wait_recv()
        block = halves(pick(after))[1]
        copies.append(wire.put(block, block, me.along(axis, before)))
    yield
    arrive(copies)


def reduce_ring(me, wire, axis, pick, far, near, out):
    t, n = me.mine(axis), me.side
    after, before = lax.rem(t + 1, n), lax.rem(t + n - 1, n)
    if n == 2:
        copies = [wire.put(pick(after), near.at[0], me.along(axis, after))]
    else:
        up, down = me.along(axis, after), me.along(axis, before)
        cross = halves(pick(lax.rem(t + 2, n)))
        to_up, to_down = halves(pick(after)), halves(pick(before))
        at_up, at_down = halves(near.at[0]), halves(near.at[1])
        first = [wire.put(cross[0], far.at[0], up), wire.put(cross[1], far.at[1], down)]
        copies = [wire.put(to_up[1], at_up[1], up), wire.put(to_down[0], at_down[0], down)]
        yield
        first[0].wait_recv()
        to_up[0][...] += far[0]
        copies.append(wire.put(to_up[0], at_up[0], up))
        first[1].wait_recv()
        to_down[1][...] += far[1]
        copies.append(wire.put(to_down[1], at_down[1], down))
    yield
    arrive(copies)
    out[...] = pick(t)[...] + near[0] if n == 2 else pick(t)[...] + near[0] + near[1]


def gather_direct(me, wire, axis, pick):
    mine = pick(me.mine(axis))
    copies = [wire.put(mine, mine, me.along(axis, t)) for _, t in me.others(axis)]
    yield
    arrive(copies)


def reduce_direct(me, wire, axis, pick, near, out):
    copies = [wire.put(pick(t), near.at[o - 1], me.along(axis, t)) for o, t in me.others(axis)]
    yield
    arrive(copies)
    total = pick(me.mine(axis))[...]
    for o in range(me.side - 1):
        total = total + near[o]
    out[...] = total


def together(*parts):
    parts = list(parts)
    while parts:
        for part in list(parts):
            if next(part, parts) is parts:
                parts.remove(part)


def arrive(copies):
    for copy in copies:
        copy.wait_recv()


def hops(depth, layer):
    far, near = depth // 2, depth - 1 - depth // 2
    return (far, near) if layer % 2 == 0 else (near, far)


def staged(parts):
    while parts:
        for part in list(parts):
            if next(part, parts) is parts:
                parts.remove(part)
        if parts:
            yield


def eye_block():
    row = lax.broadcasted_iota(jnp.int32, (NB, NB), 0)
    return (row == lax.broadcasted_iota(jnp.int32, (NB, NB), 1)).astype(F32)


def take_block(ref, n):
    piece, side = ref.shape[-2], ref.shape[1]
    parts, done = [], 0
    while done < NB:
        index, offset = (n * NB + done) // piece, (n * NB + done) % piece
        rows = min(piece - offset, NB - done)
        parts.append(ref[index // (side * side), index // side % side, index % side, offset : offset + rows])
        done += rows
    return jnp.concatenate(parts, axis=0)


def place_block(ref, n, block):
    piece = ref.shape[-2]
    flat, side = n * NB, ref.shape[1]
    done = 0
    while done < NB:
        index, offset = (flat + done) // piece, (flat + done) % piece
        rows = min(piece - offset, NB - done)
        ref[index // (side * side), index // side % side, index % side, offset : offset + rows] = block[done : done + rows]
        done += rows


def leaf_inverse(x):
    groups = NB // 8
    rows = [x[8 * g : 8 * g + 8, :] for g in range(groups)]
    lane = lax.broadcasted_iota(jnp.int32, (8, NB), 1)
    sub = lax.broadcasted_iota(jnp.int32, (8, NB), 0)
    splat = lambda v, p: jnp.broadcast_to(v[p : p + 1, :], (8, NB))
    out = []
    for g in range(groups):
        base = 8 * g
        inside = (lane >= base) & (lane < base + 8)
        cur = rows[g]
        cols = [jnp.broadcast_to(cur[:, base + q : base + q + 1], (8, NB)) for q in range(8)]
        fwd = jnp.where(inside, jnp.where(lane == sub + base, 1.0, 0.0), cur)
        full = fwd
        pivot = None
        for p in range(8):
            d = splat(cols[p], p)
            inv = 1.0 / d
            m = cols[p] * inv
            mf = jnp.where(sub > p, m, 0.0)
            mj = jnp.where(sub == p, 0.0, m)
            pivot = d if p == 0 else jnp.where(sub == p, d, pivot)
            ipivot = inv if p == 0 else jnp.where(sub == p, inv, ipivot)
            if p < 7:
                fwd = fwd - mf * splat(fwd, p)
            full = full - mj * splat(full, p)
            for q in range(p + 1, 8):
                cols[q] = cols[q] - mj * splat(cols[q], p)
        out.append(jnp.where(lane < base + 8, fwd * lax.rsqrt(pivot), 0.0))
        if g + 1 < groups:
            full = full * ipivot
            parts = [splat(full, q) for q in range(8)]
            for i in range(g + 1, groups):
                r = rows[i]
                acc = jnp.where(inside, 0.0, r)
                for q in range(8):
                    acc = acc - jnp.broadcast_to(r[:, base + q : base + q + 1], (8, NB)) * parts[q]
                rows[i] = acc
    return jnp.concatenate(out, axis=0)

def interleave(main, sides, every):
    count = 0
    for _ in main:
        count += 1
        if count % every == 0:
            for side in sides:
                next(side, None)
    for side in sides:
        for _ in side:
            pass


def dion_kernel(layers, side, depth, q_ref, m_hbm, all_ref, rb_ref, s_ref, new_ref, m_ref, qall, part, chain, p_ref, pcore, a_ref, near_a, b_ref, near_b, t_ref, s3, g_ref, wall, rt, rc, far1, near1, u, near2, tot, sq, sz, send, recv, load):
    me = Place(side, depth)
    wire = Wire(send, recv)
    x, y, c, z = me.x, me.y, me.c, me.z
    rank = p_ref.shape[-1]
    rows = part.shape[2]
    width = m_ref.shape[-1]
    blocks = rank // NB
    loads = [pltpu.make_async_copy(m_hbm.at[l], m_ref.at[l], load.at[l]) for l in range(layers)]
    for copy in loads:
        copy.start()
    qall[:, x, y, c] = q_ref[...]
    me.barrier()

    def factor_rows(l):
        yield from gather_direct(me, wire, l, lambda t: qall.at[l, t, y, c] if l == 0 else qall.at[l, x, t, c])
        yield from gather_direct(me, wire, 1 - l, lambda t: qall.at[l, :, t, c] if l == 0 else qall.at[l, t, :, c])
        crossing.append(wire.put(qall.at[l, :, :, c], qall.at[l, :, :, c], me.at(c=1 - c)))

    crossing = []
    together(*[factor_rows(l) for l in range(layers)])

    right, left = lax.rem(z + 1, depth), lax.rem(z + depth - 1, depth)

    def chain_step(l, way, s):
        count = hops(depth, l)[way]
        ahead = count - s + 1
        dest = lax.rem(z + ahead, depth) if way == 0 else lax.rem(z + depth - ahead, depth)
        src = part.at[l, dest]
        if s > 1:
            src = chain.at[l, way, s - 2]
            src[...] += part[l, dest]
        return wire.put(src, chain.at[l, way, s - 1], me.at(z=right if way == 0 else left))

    pending = {}
    for l in range(layers):
        crossing[l].wait_recv()
        loads[l].wait()
        factor = qall[l].reshape(rank, -1)

        @pl.loop(0, depth // 2)
        def _(i):
            lhs = m_ref[l, pl.ds(pl.multiple_of(i * 2 * rows, 16), 2 * rows), :]
            out = lax.dot_general(lhs, factor, (((1,), (1,)), ((), ())), preferred_element_type=F32)
            part[l, pl.ds(2 * i, 2)] = out.reshape(2, rows, rank)

        for way in (0, 1):
            if hops(depth, l)[way]:
                pending[l, way] = chain_step(l, way, 1)
    for s in range(2, depth // 2 + 1):
        for l in range(layers):
            for way in (0, 1):
                if s <= hops(depth, l)[way]:
                    pending[l, way].wait_recv()
                    pending[l, way] = chain_step(l, way, s)
    for l in range(layers):
        total = part[l, z]
        for way in (0, 1):
            count = hops(depth, l)[way]
            if count:
                pending[l, way].wait_recv()
                total = total + chain[l, way, count - 1]
        p_ref[l, z] = total

    def gather_project(l):
        pending = {}
        for s in range(1, depth // 2 + 1):
            for way in (0, 1):
                if s <= hops(depth, l)[way]:
                    if s > 1:
                        pending[way].wait_recv()
                    src = lax.rem(z + depth - (s - 1), depth) if way == 0 else lax.rem(z + s - 1, depth)
                    block = p_ref.at[l, src]
                    pending[way] = wire.put(block, block, me.at(z=right if way == 0 else left))
            yield
        arrive(list(pending.values()))

    def sum_plane(h):
        yield from reduce_direct(me, wire, h, lambda t: a_ref.at[h, t], near_a.at[h], b_ref.at[h])
        yield from reduce_direct(me, wire, 1 - h, lambda t: b_ref.at[h, t], near_b.at[h], t_ref.at[h])

    def spread_plane(h):
        i = me.mine(h)
        yield from gather_direct(me, wire, 1 - h, lambda t: g_ref.at[h, i, t])
        yield from gather_direct(me, wire, h, lambda t: g_ref.at[h, t])

    def sum_gram_and_invert():
        swap = wire.put(p_ref.at[1 - c, z], pcore, me.at(c=1 - c))
        for l in range(layers):
            next(sides[l])
        swap.wait_recv()
        both = jnp.concatenate([p_ref[c, z], pcore[...]], axis=0)
        n = 0
        for i in range(blocks):
            gram = lax.dot_general(both[:, i * NB : i * NB + NB], both[:, i * NB :], (((0,), (0,)), ((), ())), precision=HI, preferred_element_type=F32)
            for j in range(blocks - i):
                place_block(a_ref, n, gram[:, j * NB : j * NB + NB])
                n += 1
        yield from staged([sum_plane(0), sum_plane(1)])
        copies = [wire.put(t_ref, s3.at[o - 1], me.at(z=t)) for o, t in me.others_z()]
        yield
        arrive(copies)
        total = t_ref[...]
        for o in range(depth - 1):
            total = total + s3[o]
        for h in (0, 1):
            g_ref[h, me.mine(h), me.mine(1 - h)] = total[h]
        yield from staged([spread_plane(0), spread_plane(1)])
        wall[c] = jnp.zeros(wall.shape[1:], F32)
        n = 0
        for i in range(blocks):
            for j in range(i, blocks):
                wall[c, i * NB : i * NB + NB, j * NB : j * NB + NB] = take_block(g_ref, n)
                n += 1
        ident = eye_block()
        for k in range(blocks):
            yield
            sl = slice(k * NB, k * NB + NB)
            w = leaf_inverse(wall[c, sl, sl])
            colid = lax.broadcasted_iota(jnp.int32, (NB, rank), 1) // NB
            row = jnp.where(colid == k, jnp.concatenate([ident] * blocks, axis=1), wall[c, sl, :])
            out = jnp.dot(w, row, precision=HI, preferred_element_type=F32)
            wall[c, sl, :] = jnp.where(colid <= k, out, 0.0)
            if k + 1 < blocks:
                tail = slice(k * NB + NB, rank)
                upd = lax.dot_general(out[:, k * NB + NB :], out, (((0,), (0,)), ((), ())), precision=HI, preferred_element_type=F32)
                keep = wall[c, tail, :]
                cid = lax.broadcasted_iota(jnp.int32, keep.shape, 1) // NB
                wall[c, tail, :] = jnp.where(cid == k, 0.0, keep) - upd

    sides = [gather_project(l) for l in range(layers)]
    interleave(sum_gram_and_invert(), sides, 3)
    wire.put(wall.at[c], wall.at[c], me.at(c=1 - c)).wait_recv()

    def sum_rows(l):
        core = wire.put(rt.at[l, :, :, 1 - c], rc.at[l], me.at(c=1 - c))
        yield
        core.wait_recv()
        rc[l] += rt[l, :, :, c]
        pick = lambda t: rc.at[l, t] if l == 0 else rc.at[l, :, t]
        yield from reduce_ring(me, wire, l, pick, far1.at[l], near1.at[l], u.at[l])
        yield from reduce_direct(me, wire, 1 - l, lambda t: u.at[l, t], near2.at[l], tot.at[l])

    sums = []
    for l in range(layers):
        w_high = wall[l].astype(BF16)
        w_low = (wall[l] - w_high.astype(F32)).astype(BF16)

        @pl.loop(0, depth // 2)
        def _(i):
            lhs = p_ref[l, pl.ds(2 * i, 2)].reshape(-1, rank)
            high = lhs.astype(BF16)
            low = (lhs - high.astype(F32)).astype(BF16)
            dot = lambda a, b: lax.dot_general(a, b, (((1,), (1,)), ((), ())), preferred_element_type=F32)
            out = dot(high, w_high) + (dot(high, w_low) + dot(low, w_high))
            all_ref[l, pl.ds(2 * i, 2)] = out.astype(BF16).reshape(2, -1, rank)

        for part_sum in sums:
            next(part_sum)
        ortho = all_ref[l].reshape(-1, rank)
        for k in range(width // 256):
            cols = slice(256 * k, 256 * k + 256)
            out = lax.dot_general(ortho, m_ref[l, :, cols], (((0,), (0,)), ((), ())), preferred_element_type=F32)
            rt[l, :, :, :, :, cols] = out.reshape(rt.shape[1:5] + (256,))
        sums.append(sum_rows(l))
        next(sums[l])
    together(*sums)

    def gather_rows(l):
        rb_ref[l, x, y, c] = tot[l].astype(BF16)
        yield from gather_direct(me, wire, l, lambda t: rb_ref.at[l, t, y, c] if l == 0 else rb_ref.at[l, x, t, c])
        yield from gather_direct(me, wire, 1 - l, lambda t: rb_ref.at[l, :, t, c] if l == 0 else rb_ref.at[l, t, :, c])
        cross = wire.put(rb_ref.at[l, :, :, c], rb_ref.at[l, :, :, c], me.at(c=1 - c))
        yield
        cross.wait_recv()

    def gather_norms():
        for l in range(layers):
            sq[l] = jnp.broadcast_to(jnp.sum(tot[l] * tot[l], axis=1, keepdims=True), sq.shape[1:])
        copies = [wire.put(sq, sz.at[o - 1], me.at(z=t)) for o, t in me.others_z()]
        yield
        arrive(copies)
        norm = sq[...]
        for o in range(depth - 1):
            norm = norm + sz[o]
        factor = lax.rsqrt(norm + 1e-06)
        for l in range(layers):
            s_ref[l, x, y, c] = factor[l]
            new_ref[l] = (tot[l] * factor[l, :, :1]).astype(BF16)
        mine = s_ref.at[:, x, y, c]
        copies = [wire.put(mine, mine, me.along(0, t)) for _, t in me.others(0)]
        yield
        arrive(copies)
        mine = s_ref.at[:, :, y, c]
        copies = [wire.put(mine, mine, me.along(1, t)) for _, t in me.others(1)]
        yield
        arrive(copies)
        copies = [wire.put(s_ref.at[:, :, :, c], s_ref.at[:, :, :, c], me.at(c=1 - c))]
        yield
        arrive(copies)

    together(*[gather_rows(l) for l in range(layers)], gather_norms())
    wire.finish()


def dion(momentum, factor, side, depth):
    layers, rows, width = momentum.shape
    per = factor.shape[1]
    rank = per * side * side * CORES
    short = rows // depth
    blocks = rank // NB
    piece = blocks * (blocks + 1) // 2 * NB // (2 * side * side)
    whole = (2, side, side, piece, NB)
    grid = (side, side, CORES, per)
    ortho, rb, s, new = pl.pallas_call(
        functools.partial(dion_kernel, layers, side, depth),
        out_shape=(
            jax.ShapeDtypeStruct((layers, depth, short, rank), BF16),
            jax.ShapeDtypeStruct((layers,) + grid + (width,), BF16),
            jax.ShapeDtypeStruct((layers,) + grid + (128,), F32),
            jax.ShapeDtypeStruct((layers, per, width), BF16),
        ),
        in_specs=[pl.BlockSpec(memory_space=pltpu.VMEM), pl.BlockSpec(memory_space=pl.ANY)],
        out_specs=[pl.BlockSpec(memory_space=pltpu.VMEM)] * 4,
        scratch_shapes=[
            pltpu.VMEM(momentum.shape, BF16),
            pltpu.VMEM((layers,) + grid + (width,), BF16),
            pltpu.VMEM((layers, depth, short, rank), F32),
            pltpu.VMEM((layers, 2, max(1, depth // 2), short, rank), F32),
            pltpu.VMEM((layers, depth, short, rank), F32),
            pltpu.VMEM((short, rank), F32),
            pltpu.VMEM(whole, F32),
            pltpu.VMEM((2, side - 1) + whole[2:], F32),
            pltpu.VMEM((2,) + whole[2:], F32),
            pltpu.VMEM((2, side - 1) + whole[3:], F32),
            pltpu.VMEM((2,) + whole[3:], F32),
            pltpu.VMEM((depth - 1, 2) + whole[3:], F32),
            pltpu.VMEM(whole, F32),
            pltpu.VMEM((layers, rank, rank), F32),
            pltpu.VMEM((layers,) + grid + (width,), F32),
            pltpu.VMEM((layers, side, side, per, width), F32),
            pltpu.VMEM((layers, 2, side, per, width // 2), F32),
            pltpu.VMEM((layers, 2, side, per, width), F32),
            pltpu.VMEM((layers, side, per, width), F32),
            pltpu.VMEM((layers, side - 1, per, width), F32),
            pltpu.VMEM((layers, per, width), F32),
            pltpu.VMEM((layers, per, 128), F32),
            pltpu.VMEM((depth - 1, layers, per, 128), F32),
            pltpu.SemaphoreType.DMA((160,)),
            pltpu.SemaphoreType.DMA((160,)),
            pltpu.SemaphoreType.DMA((layers,)),
        ],
        compiler_params=pltpu.CompilerParams(collective_id=0, has_side_effects=True, vmem_limit_bytes=VMEM_BYTES),
        name="dion",
    )(factor, momentum)
    return ortho.reshape(layers, rows, rank), rb.reshape(layers, rank, width), s.reshape(layers, rank, 128), new


def final_kernel(scale, o_ref, m_ref, rb_ref, s_ref, mom_ref, up_ref):
    ortho, rb = o_ref[0], rb_ref[0]
    feedback = jnp.dot(ortho, rb, preferred_element_type=F32)
    mom_ref[0] = (m_ref[0].astype(F32) - 0.05 * feedback).astype(BF16)
    normed = (rb.astype(F32) * s_ref[0, :, :1]).astype(BF16)
    up_ref[0] = (scale * jnp.dot(ortho, normed, preferred_element_type=F32)).astype(BF16)


def final_products(ortho, momentum, rb, s, scale):
    layers, rows, rank = ortho.shape
    width = momentum.shape[-1]
    block = min(width, 256)
    cols = lambda n: pl.BlockSpec((1, n, block), lambda l, i: (l, 0, i))
    full = lambda n, w: pl.BlockSpec((1, n, w), lambda l, i: (l, 0, 0))
    return pl.pallas_call(
        functools.partial(final_kernel, scale),
        grid=(layers, width // block),
        out_shape=[jax.ShapeDtypeStruct(momentum.shape, BF16)] * 2,
        in_specs=[full(rows, rank), cols(rows), cols(rank), full(rank, 128)],
        out_specs=[cols(rows)] * 2,
        compiler_params=pltpu.CompilerParams(vmem_limit_bytes=VMEM_BYTES),
        name="final_products",
    )(ortho, momentum, rb, s)


def solution(mesh):
    side = math.isqrt(mesh.shape["fsdp"] // CORES)
    depth = mesh.shape["tp"]

    def local(momentum, right_factor):
        rank = right_factor.shape[1] * side * side * CORES
        total_rows, total_cols = momentum.shape[1] * side * side * CORES, momentum.shape[2] * depth
        scale = math.sqrt(total_rows * total_cols / rank)
        ortho, rb, s, new_factor = dion(momentum, right_factor, side, depth)
        new_momentum, update = final_products(ortho, momentum, rb, s, scale)
        return new_momentum, update, new_factor

    spec = P(None, "fsdp", "tp")
    return jax.shard_map(local, mesh=mesh, in_specs=(spec, spec), out_specs=(spec, spec, spec), check_vma=False)
```

```python
import functools
import math

import jax
import jax.numpy as jnp
from jax import lax
from jax.experimental import pallas as pl
from jax.experimental.pallas import tpu as pltpu
from jax.sharding import PartitionSpec as P

MESH = pl.DeviceIdType.MESH
HI = lax.Precision.HIGHEST
CORES = 2
NB = 128
SPAN = 4
VMEM_BYTES = 48 * 2**20
F32 = jnp.float32
BF16 = jnp.bfloat16


class Place:
    def __init__(self, side, depth):
        f, self.z = lax.axis_index("fsdp"), lax.axis_index("tp")
        self.side, self.depth = side, depth
        self.x, self.y, self.c = f // (side * CORES), (f // CORES) % side, f % CORES

    def at(self, x=None, y=None, c=None, z=None):
        x = self.x if x is None else x
        y = self.y if y is None else y
        c = self.c if c is None else c
        z = self.z if z is None else z
        return ((x * self.side + y) * CORES + c, z)

    def along(self, axis, t):
        return self.at(x=t) if axis == 0 else self.at(y=t)

    def mine(self, axis):
        return self.x if axis == 0 else self.y

    def others(self, axis):
        return [(o, lax.rem(self.mine(axis) + o, self.side)) for o in range(1, self.side)]

    def others_z(self):
        return [(o, lax.rem(self.z + o, self.depth)) for o in range(1, self.depth)]

    def barrier(self):
        sem = pltpu.get_barrier_semaphore()
        devices = [self.at(c=1 - self.c)]
        devices += [self.along(a, t) for a in (0, 1) for _, t in self.others(a)]
        devices += [self.at(z=t) for _, t in self.others_z()]
        for device in devices:
            pl.semaphore_signal(sem, inc=1, device_id=device, device_id_type=MESH)
        pl.semaphore_wait(sem, len(devices))


class Wire:
    def __init__(self, send, recv):
        self.send, self.recv, self.used, self.copies = send, recv, 0, []

    def put(self, src, dst, device):
        n = self.used
        self.used += 1
        copy = pltpu.make_async_remote_copy(
            src_ref=src,
            dst_ref=dst,
            send_sem=self.send.at[n],
            recv_sem=self.recv.at[n],
            device_id=device,
            device_id_type=MESH,
        )
        copy.start()
        self.copies.append(copy)
        return copy

    def finish(self):
        for copy in self.copies:
            copy.wait_send()


def halves(ref):
    wide = ref.shape[-1] // 2
    lead = (slice(None),) * (len(ref.shape) - 1)
    return ref.at[lead + (slice(0, wide),)], ref.at[lead + (slice(wide, 2 * wide),)]


def gather_ring(me, wire, axis, pick):
    t, n = me.mine(axis), me.side
    after, before = lax.rem(t + 1, n), lax.rem(t + n - 1, n)
    if n == 2:
        copies = [wire.put(pick(t), pick(t), me.along(axis, after))]
    else:
        up = wire.put(pick(t), pick(t), me.along(axis, after))
        down = wire.put(pick(t), pick(t), me.along(axis, before))
        yield
        up.wait_recv()
        block = halves(pick(before))[0]
        copies = [wire.put(block, block, me.along(axis, after))]
        down.wait_recv()
        block = halves(pick(after))[1]
        copies.append(wire.put(block, block, me.along(axis, before)))
    yield
    arrive(copies)


def reduce_ring(me, wire, axis, pick, far, near, out):
    t, n = me.mine(axis), me.side
    after, before = lax.rem(t + 1, n), lax.rem(t + n - 1, n)
    if n == 2:
        copies = [wire.put(pick(after), near.at[0], me.along(axis, after))]
    else:
        up, down = me.along(axis, after), me.along(axis, before)
        cross = halves(pick(lax.rem(t + 2, n)))
        to_up, to_down = halves(pick(after)), halves(pick(before))
        at_up, at_down = halves(near.at[0]), halves(near.at[1])
        first = [wire.put(cross[0], far.at[0], up), wire.put(cross[1], far.at[1], down)]
        copies = [wire.put(to_up[1], at_up[1], up), wire.put(to_down[0], at_down[0], down)]
        yield
        first[0].wait_recv()
        to_up[0][...] += far[0]
        copies.append(wire.put(to_up[0], at_up[0], up))
        first[1].wait_recv()
        to_down[1][...] += far[1]
        copies.append(wire.put(to_down[1], at_down[1], down))
    yield
    arrive(copies)
    out[...] = pick(t)[...] + near[0] if n == 2 else pick(t)[...] + near[0] + near[1]


def gather_direct(me, wire, axis, pick):
    mine = pick(me.mine(axis))
    copies = [wire.put(mine, mine, me.along(axis, t)) for _, t in me.others(axis)]
    yield
    arrive(copies)


def reduce_direct(me, wire, axis, pick, near, out):
    copies = [wire.put(pick(t), near.at[o - 1], me.along(axis, t)) for o, t in me.others(axis)]
    yield
    arrive(copies)
    total = pick(me.mine(axis))[...]
    for o in range(me.side - 1):
        total = total + near[o]
    out[...] = total


def together(*parts):
    parts = list(parts)
    while parts:
        for part in list(parts):
            if next(part, parts) is parts:
                parts.remove(part)


def arrive(copies):
    for copy in copies:
        copy.wait_recv()


def hops(depth, layer):
    far, near = depth // 2, depth - 1 - depth // 2
    return (far, near) if layer % 2 == 0 else (near, far)


def staged(parts):
    while parts:
        for part in list(parts):
            if next(part, parts) is parts:
                parts.remove(part)
        if parts:
            yield


def eye_block():
    row = lax.broadcasted_iota(jnp.int32, (NB, NB), 0)
    return (row == lax.broadcasted_iota(jnp.int32, (NB, NB), 1)).astype(F32)


def take_block(ref, n):
    piece, side = ref.shape[-2], ref.shape[1]
    parts, done = [], 0
    while done < NB:
        index, offset = (n * NB + done) // piece, (n * NB + done) % piece
        rows = min(piece - offset, NB - done)
        parts.append(ref[index // (side * side), index // side % side, index % side, offset : offset + rows])
        done += rows
    return jnp.concatenate(parts, axis=0)


def place_block(ref, n, block):
    piece = ref.shape[-2]
    flat, side = n * NB, ref.shape[1]
    done = 0
    while done < NB:
        index, offset = (flat + done) // piece, (flat + done) % piece
        rows = min(piece - offset, NB - done)
        ref[index // (side * side), index // side % side, index % side, offset : offset + rows] = block[done : done + rows]
        done += rows


def leaf_inverse(x):
    groups = NB // 8
    rows = [x[8 * g : 8 * g + 8, :] for g in range(groups)]
    lane = lax.broadcasted_iota(jnp.int32, (8, NB), 1)
    sub = lax.broadcasted_iota(jnp.int32, (8, NB), 0)
    splat = lambda v, p: jnp.broadcast_to(v[p : p + 1, :], (8, NB))
    out = []
    for g in range(groups):
        base = 8 * g
        inside = (lane >= base) & (lane < base + 8)
        cur = rows[g]
        cols = [jnp.broadcast_to(cur[:, base + q : base + q + 1], (8, NB)) for q in range(8)]
        fwd = jnp.where(inside, jnp.where(lane == sub + base, 1.0, 0.0), cur)
        full = fwd
        last = (g + 1) % SPAN == 0
        for p in range(8):
            d = splat(cols[p], p)
            inv = 1.0 / d
            m = cols[p] * inv
            mf = jnp.where(sub > p, m, 0.0)
            pivot = d if p == 0 else jnp.where(sub == p, d, pivot)
            ipivot = inv if p == 0 else jnp.where(sub == p, inv, ipivot)
            if p < 7:
                fwd = fwd - mf * splat(fwd, p)
            if not last:
                mj = jnp.where(sub == p, 0.0, m)
                full = full - mj * splat(full, p)
            for q in range(p + 1, 8):
                cols[q] = cols[q] - (mf if last else mj) * splat(cols[q], p)
        y = fwd * lax.rsqrt(pivot)
        out.append(y)
        if last:
            if g + 1 < groups:
                first = g + 1 - SPAN
                block = jnp.concatenate(out[first : g + 1], axis=0)
                right = jnp.concatenate([jnp.where((lane >= 8 * f + 8) & (lane < base + 8), 0.0, out[f]) for f in range(first, g + 1)], axis=0)
                upd = lax.dot_general(block, right, (((0,), (0,)), ((), ())), precision=HI, preferred_element_type=F32)
                gone = (lane >= 8 * first) & (lane < base + 8)
                for i in range(g + 1, groups):
                    rows[i] = jnp.where(gone, 0.0, rows[i]) - upd[8 * i : 8 * i + 8, :]
        else:
            full = full * ipivot
            parts = [splat(full, q) for q in range(8)]
            for i in range(g + 1, g + 1 - (g + 1) % SPAN + SPAN):
                r = rows[i]
                acc = jnp.where(inside, 0.0, r)
                for q in range(8):
                    acc = acc - jnp.broadcast_to(r[:, base + q : base + q + 1], (8, NB)) * parts[q]
                rows[i] = acc
    return jnp.concatenate([jnp.where(lane < 8 * g + 8, y, 0.0) for g, y in enumerate(out)], axis=0)


def interleave(main, sides, turns):
    count = 0
    for _ in main:
        count += 1
        if count in turns:
            for side in sides:
                next(side, None)
    for side in sides:
        for _ in side:
            pass


def dion_kernel(layers, side, depth, q_ref, m_hbm, all_ref, rb_ref, s_ref, new_ref, m_ref, qall, part, chain, p_ref, pcore, a_ref, near_a, b_ref, near_b, t_ref, s3, g_ref, wall, rt, rc, far1, near1, u, near2, tot, sq, sz, qt, wt, send, recv, load):
    me = Place(side, depth)
    wire = Wire(send, recv)
    x, y, c, z = me.x, me.y, me.c, me.z
    rank = p_ref.shape[-1]
    rows = part.shape[2]
    width = m_ref.shape[-1]
    blocks = rank // NB
    loads = [pltpu.make_async_copy(m_hbm.at[l], m_ref.at[l], load.at[l]) for l in range(layers)]
    for copy in loads:
        copy.start()
    qall[:, x, y, c] = q_ref[...]
    me.barrier()

    def factor_rows(l):
        yield from gather_direct(me, wire, l, lambda t: qall.at[l, t, y, c] if l == 0 else qall.at[l, x, t, c])
        yield from gather_direct(me, wire, 1 - l, lambda t: qall.at[l, :, t, c] if l == 0 else qall.at[l, t, :, c])
        crossing.append(wire.put(qall.at[l, :, :, c], qall.at[l, :, :, c], me.at(c=1 - c)))

    crossing = []
    together(*[factor_rows(l) for l in range(layers)])

    right, left = lax.rem(z + 1, depth), lax.rem(z + depth - 1, depth)

    def chain_step(l, way, s):
        count = hops(depth, l)[way]
        ahead = count - s + 1
        dest = lax.rem(z + ahead, depth) if way == 0 else lax.rem(z + depth - ahead, depth)
        src = part.at[l, dest]
        if s > 1:
            src = chain.at[l, way, s - 2]
            src[...] += part[l, dest]
        return wire.put(src, chain.at[l, way, s - 1], me.at(z=right if way == 0 else left))

    pending = {}
    for l in range(layers):
        crossing[l].wait_recv()
        loads[l].wait()
        qt[...] = jnp.transpose(qall[l].reshape(rank, -1))

        @pl.loop(0, depth // 2)
        def _(i):
            lhs = m_ref[l, pl.ds(pl.multiple_of(i * 2 * rows, 16), 2 * rows), :]
            out = jnp.dot(lhs, qt[...], preferred_element_type=F32)
            part[l, pl.ds(2 * i, 2)] = out.reshape(2, rows, rank)

        for way in (0, 1):
            if hops(depth, l)[way]:
                pending[l, way] = chain_step(l, way, 1)
    for s in range(2, depth // 2 + 1):
        for l in range(layers):
            for way in (0, 1):
                if s <= hops(depth, l)[way]:
                    pending[l, way].wait_recv()
                    pending[l, way] = chain_step(l, way, s)
    for l in range(layers):
        total = part[l, z]
        for way in (0, 1):
            count = hops(depth, l)[way]
            if count:
                pending[l, way].wait_recv()
                total = total + chain[l, way, count - 1]
        p_ref[l, z] = total

    def gather_project(l):
        pending = {}
        for s in range(1, depth // 2 + 1):
            for way in (0, 1):
                if s <= hops(depth, l)[way]:
                    if s > 1:
                        pending[way].wait_recv()
                    src = lax.rem(z + depth - (s - 1), depth) if way == 0 else lax.rem(z + s - 1, depth)
                    block = p_ref.at[l, src]
                    pending[way] = wire.put(block, block, me.at(z=right if way == 0 else left))
            yield
        arrive(list(pending.values()))

    def sum_plane(h):
        yield from reduce_direct(me, wire, h, lambda t: a_ref.at[h, t], near_a.at[h], b_ref.at[h])
        yield from reduce_direct(me, wire, 1 - h, lambda t: b_ref.at[h, t], near_b.at[h], t_ref.at[h])

    def spread_plane(h):
        i = me.mine(h)
        yield from gather_direct(me, wire, 1 - h, lambda t: g_ref.at[h, i, t])
        yield from gather_direct(me, wire, h, lambda t: g_ref.at[h, t])

    def sum_gram_and_invert():
        swap = wire.put(p_ref.at[1 - c, z], pcore, me.at(c=1 - c))
        for l in range(layers):
            next(sides[l])
        swap.wait_recv()
        both = jnp.concatenate([p_ref[c, z], pcore[...]], axis=0)
        n = 0
        for i in range(blocks):
            gram = lax.dot_general(both[:, i * NB : i * NB + NB], both[:, i * NB :], (((0,), (0,)), ((), ())), precision=HI, preferred_element_type=F32)
            for j in range(blocks - i):
                place_block(a_ref, n, gram[:, j * NB : j * NB + NB])
                n += 1
        yield from staged([sum_plane(0), sum_plane(1)])
        copies = [wire.put(t_ref, s3.at[o - 1], me.at(z=t)) for o, t in me.others_z()]
        yield
        arrive(copies)
        total = t_ref[...]
        for o in range(depth - 1):
            total = total + s3[o]
        for h in (0, 1):
            g_ref[h, me.mine(h), me.mine(1 - h)] = total[h]
        yield from staged([spread_plane(0), spread_plane(1)])
        wall[c] = jnp.zeros(wall.shape[1:], F32)
        n = 0
        for i in range(blocks):
            for j in range(i, blocks):
                wall[c, i * NB : i * NB + NB, j * NB : j * NB + NB] = take_block(g_ref, n)
                n += 1
        ident = eye_block()
        for k in range(blocks):
            yield
            sl = slice(k * NB, k * NB + NB)
            w = leaf_inverse(wall[c, sl, sl])
            colid = lax.broadcasted_iota(jnp.int32, (NB, rank), 1) // NB
            row = jnp.where(colid == k, jnp.concatenate([ident] * blocks, axis=1), wall[c, sl, :])
            out = jnp.dot(w, row, precision=HI, preferred_element_type=F32)
            wall[c, sl, :] = jnp.where(colid <= k, out, 0.0)
            if k + 1 < blocks:
                tail = slice(k * NB + NB, rank)
                upd = lax.dot_general(out[:, k * NB + NB :], out, (((0,), (0,)), ((), ())), precision=HI, preferred_element_type=F32)
                keep = wall[c, tail, :]
                cid = lax.broadcasted_iota(jnp.int32, keep.shape, 1) // NB
                wall[c, tail, :] = jnp.where(cid == k, 0.0, keep) - upd

    sides = [gather_project(l) for l in range(layers)]
    interleave(sum_gram_and_invert(), sides, (3, 5, 7))
    wire.put(wall.at[c], wall.at[c], me.at(c=1 - c)).wait_recv()

    def sum_rows(l):
        core = wire.put(rt.at[l, :, :, 1 - c], rc.at[l], me.at(c=1 - c))
        yield
        core.wait_recv()
        rc[l] += rt[l, :, :, c]
        pick = lambda t: rc.at[l, t] if l == 0 else rc.at[l, :, t]
        yield from reduce_ring(me, wire, l, pick, far1.at[l], near1.at[l], u.at[l])
        yield from reduce_direct(me, wire, 1 - l, lambda t: u.at[l, t], near2.at[l], tot.at[l])

    sums = []
    for l in range(layers):
        turned = jnp.transpose(wall[l])
        wt[0] = turned.astype(BF16)
        wt[1] = (turned - turned.astype(BF16).astype(F32)).astype(BF16)

        @pl.loop(0, depth // 2)
        def _(i):
            lhs = p_ref[l, pl.ds(2 * i, 2)].reshape(-1, rank)
            high = lhs.astype(BF16)
            low = (lhs - high.astype(F32)).astype(BF16)
            dot = lambda a, b: jnp.dot(a, b, preferred_element_type=F32)
            out = dot(high, wt[0]) + (dot(high, wt[1]) + dot(low, wt[0]))
            all_ref[l, pl.ds(2 * i, 2)] = out.astype(BF16).reshape(2, -1, rank)

        for part_sum in sums:
            next(part_sum)
        ortho = all_ref[l].reshape(-1, rank)
        for k in range(width // 256):
            cols = slice(256 * k, 256 * k + 256)
            out = lax.dot_general(ortho, m_ref[l, :, cols], (((0,), (0,)), ((), ())), preferred_element_type=F32)
            rt[l, :, :, :, :, cols] = out.reshape(rt.shape[1:5] + (256,))
        sums.append(sum_rows(l))
        next(sums[l])
    together(*sums)

    def gather_rows(l):
        rb_ref[l, x, y, c] = tot[l].astype(BF16)
        yield from gather_direct(me, wire, l, lambda t: rb_ref.at[l, t, y, c] if l == 0 else rb_ref.at[l, x, t, c])
        yield from gather_direct(me, wire, 1 - l, lambda t: rb_ref.at[l, :, t, c] if l == 0 else rb_ref.at[l, t, :, c])
        cross = wire.put(rb_ref.at[l, :, :, c], rb_ref.at[l, :, :, c], me.at(c=1 - c))
        yield
        cross.wait_recv()

    def gather_norms():
        for l in range(layers):
            sq[l] = jnp.broadcast_to(jnp.sum(tot[l] * tot[l], axis=1, keepdims=True), sq.shape[1:])
        copies = [wire.put(sq, sz.at[o - 1], me.at(z=t)) for o, t in me.others_z()]
        yield
        arrive(copies)
        norm = sq[...]
        for o in range(depth - 1):
            norm = norm + sz[o]
        factor = lax.rsqrt(norm + 1e-06)
        for l in range(layers):
            s_ref[l, x, y, c] = factor[l]
            new_ref[l] = (tot[l] * factor[l, :, :1]).astype(BF16)
        mine = s_ref.at[:, x, y, c]
        copies = [wire.put(mine, mine, me.along(0, t)) for _, t in me.others(0)]
        yield
        arrive(copies)
        mine = s_ref.at[:, :, y, c]
        copies = [wire.put(mine, mine, me.along(1, t)) for _, t in me.others(1)]
        yield
        arrive(copies)
        copies = [wire.put(s_ref.at[:, :, :, c], s_ref.at[:, :, :, c], me.at(c=1 - c))]
        yield
        arrive(copies)

    together(*[gather_rows(l) for l in range(layers)], gather_norms())
    wire.finish()


def dion(momentum, factor, side, depth):
    layers, rows, width = momentum.shape
    per = factor.shape[1]
    rank = per * side * side * CORES
    short = rows // depth
    blocks = rank // NB
    piece = blocks * (blocks + 1) // 2 * NB // (2 * side * side)
    whole = (2, side, side, piece, NB)
    grid = (side, side, CORES, per)
    ortho, rb, s, new = pl.pallas_call(
        functools.partial(dion_kernel, layers, side, depth),
        out_shape=(
            jax.ShapeDtypeStruct((layers, depth, short, rank), BF16),
            jax.ShapeDtypeStruct((layers,) + grid + (width,), BF16),
            jax.ShapeDtypeStruct((layers,) + grid + (128,), F32),
            jax.ShapeDtypeStruct((layers, per, width), BF16),
        ),
        in_specs=[pl.BlockSpec(memory_space=pltpu.VMEM), pl.BlockSpec(memory_space=pl.ANY)],
        out_specs=[pl.BlockSpec(memory_space=pltpu.VMEM)] * 4,
        scratch_shapes=[
            pltpu.VMEM(momentum.shape, BF16),
            pltpu.VMEM((layers,) + grid + (width,), BF16),
            pltpu.VMEM((layers, depth, short, rank), F32),
            pltpu.VMEM((layers, 2, max(1, depth // 2), short, rank), F32),
            pltpu.VMEM((layers, depth, short, rank), F32),
            pltpu.VMEM((short, rank), F32),
            pltpu.VMEM(whole, F32),
            pltpu.VMEM((2, side - 1) + whole[2:], F32),
            pltpu.VMEM((2,) + whole[2:], F32),
            pltpu.VMEM((2, side - 1) + whole[3:], F32),
            pltpu.VMEM((2,) + whole[3:], F32),
            pltpu.VMEM((depth - 1, 2) + whole[3:], F32),
            pltpu.VMEM(whole, F32),
            pltpu.VMEM((layers, rank, rank), F32),
            pltpu.VMEM((layers,) + grid + (width,), F32),
            pltpu.VMEM((layers, side, side, per, width), F32),
            pltpu.VMEM((layers, 2, side, per, width // 2), F32),
            pltpu.VMEM((layers, 2, side, per, width), F32),
            pltpu.VMEM((layers, side, per, width), F32),
            pltpu.VMEM((layers, side - 1, per, width), F32),
            pltpu.VMEM((layers, per, width), F32),
            pltpu.VMEM((layers, per, 128), F32),
            pltpu.VMEM((depth - 1, layers, per, 128), F32),
            pltpu.VMEM((width, rank), BF16),
            pltpu.VMEM((2, rank, rank), BF16),
            pltpu.SemaphoreType.DMA((160,)),
            pltpu.SemaphoreType.DMA((160,)),
            pltpu.SemaphoreType.DMA((layers,)),
        ],
        compiler_params=pltpu.CompilerParams(collective_id=0, has_side_effects=True, vmem_limit_bytes=VMEM_BYTES),
        name="dion",
    )(factor, momentum)
    return ortho.reshape(layers, rows, rank), rb.reshape(layers, rank, width), s.reshape(layers, rank, 128), new


def final_kernel(scale, o_ref, m_ref, rb_ref, s_ref, mom_ref, up_ref):
    ortho, rb = o_ref[0], rb_ref[0]
    feedback = jnp.dot(ortho, rb, preferred_element_type=F32)
    mom_ref[0] = (m_ref[0].astype(F32) - 0.05 * feedback).astype(BF16)
    normed = (rb.astype(F32) * s_ref[0, :, :1]).astype(BF16)
    up_ref[0] = (scale * jnp.dot(ortho, normed, preferred_element_type=F32)).astype(BF16)


def final_products(ortho, momentum, rb, s, scale):
    layers, rows, rank = ortho.shape
    width = momentum.shape[-1]
    block = rows // 2
    tall = lambda w: pl.BlockSpec((1, block, w), lambda l, i: (l, i, 0))
    full = lambda w: pl.BlockSpec((1, rank, w), lambda l, i: (l, 0, 0))
    return pl.pallas_call(
        functools.partial(final_kernel, scale),
        grid=(layers, 2),
        out_shape=[jax.ShapeDtypeStruct(momentum.shape, BF16)] * 2,
        in_specs=[tall(rank), tall(width), full(width), full(128)],
        out_specs=[tall(width)] * 2,
        compiler_params=pltpu.CompilerParams(vmem_limit_bytes=VMEM_BYTES),
        name="final_products",
    )(ortho, momentum, rb, s)


def solution(mesh):
    side = math.isqrt(mesh.shape["fsdp"] // CORES)
    depth = mesh.shape["tp"]

    def local(momentum, right_factor):
        rank = right_factor.shape[1] * side * side * CORES
        total_rows, total_cols = momentum.shape[1] * side * side * CORES, momentum.shape[2] * depth
        scale = math.sqrt(total_rows * total_cols / rank)
        ortho, rb, s, new_factor = dion(momentum, right_factor, side, depth)
        new_momentum, update = final_products(ortho, momentum, rb, s, scale)
        return new_momentum, update, new_factor

    spec = P(None, "fsdp", "tp")
    return jax.shard_map(local, mesh=mesh, in_specs=(spec, spec), out_specs=(spec, spec, spec), check_vma=False)
```

```python
import functools
import math

import jax
import jax.numpy as jnp
from jax import lax
from jax.experimental import pallas as pl
from jax.experimental.pallas import tpu as pltpu
from jax.sharding import PartitionSpec as P

MESH = pl.DeviceIdType.MESH
HI = lax.Precision.HIGHEST
CORES = 2
NB = 128
SPAN = 4
VMEM_BYTES = 48 * 2**20
F32 = jnp.float32
BF16 = jnp.bfloat16


class Place:
    def __init__(self, side, depth):
        f, self.z = lax.axis_index("fsdp"), lax.axis_index("tp")
        self.side, self.depth = side, depth
        self.x, self.y, self.c = f // (side * CORES), (f // CORES) % side, f % CORES

    def at(self, x=None, y=None, c=None, z=None):
        x = self.x if x is None else x
        y = self.y if y is None else y
        c = self.c if c is None else c
        z = self.z if z is None else z
        return ((x * self.side + y) * CORES + c, z)

    def along(self, axis, t):
        return self.at(x=t) if axis == 0 else self.at(y=t)

    def mine(self, axis):
        return self.x if axis == 0 else self.y

    def others(self, axis):
        return [(o, lax.rem(self.mine(axis) + o, self.side)) for o in range(1, self.side)]

    def others_z(self):
        return [(o, lax.rem(self.z + o, self.depth)) for o in range(1, self.depth)]

    def barrier(self):
        sem = pltpu.get_barrier_semaphore()
        devices = [self.at(c=1 - self.c)]
        devices += [self.along(a, t) for a in (0, 1) for _, t in self.others(a)]
        devices += [self.at(z=t) for _, t in self.others_z()]
        for device in devices:
            pl.semaphore_signal(sem, inc=1, device_id=device, device_id_type=MESH)
        pl.semaphore_wait(sem, len(devices))


class Wire:
    def __init__(self, send, recv):
        self.send, self.recv, self.used, self.copies = send, recv, 0, []

    def put(self, src, dst, device):
        n = self.used
        self.used += 1
        copy = pltpu.make_async_remote_copy(
            src_ref=src,
            dst_ref=dst,
            send_sem=self.send.at[n],
            recv_sem=self.recv.at[n],
            device_id=device,
            device_id_type=MESH,
        )
        copy.start()
        self.copies.append(copy)
        return copy

    def finish(self):
        for copy in self.copies:
            copy.wait_send()


def halves(ref):
    wide = ref.shape[-1] // 2
    lead = (slice(None),) * (len(ref.shape) - 1)
    return ref.at[lead + (slice(0, wide),)], ref.at[lead + (slice(wide, 2 * wide),)]


def gather_ring(me, wire, axis, pick):
    t, n = me.mine(axis), me.side
    after, before = lax.rem(t + 1, n), lax.rem(t + n - 1, n)
    if n == 2:
        copies = [wire.put(pick(t), pick(t), me.along(axis, after))]
    else:
        up = wire.put(pick(t), pick(t), me.along(axis, after))
        down = wire.put(pick(t), pick(t), me.along(axis, before))
        yield
        up.wait_recv()
        block = halves(pick(before))[0]
        copies = [wire.put(block, block, me.along(axis, after))]
        down.wait_recv()
        block = halves(pick(after))[1]
        copies.append(wire.put(block, block, me.along(axis, before)))
    yield
    arrive(copies)


def reduce_ring(me, wire, axis, pick, far, near, out):
    t, n = me.mine(axis), me.side
    after, before = lax.rem(t + 1, n), lax.rem(t + n - 1, n)
    if n == 2:
        copies = [wire.put(pick(after), near.at[0], me.along(axis, after))]
    else:
        up, down = me.along(axis, after), me.along(axis, before)
        cross = halves(pick(lax.rem(t + 2, n)))
        to_up, to_down = halves(pick(after)), halves(pick(before))
        at_up, at_down = halves(near.at[0]), halves(near.at[1])
        first = [wire.put(cross[0], far.at[0], up), wire.put(cross[1], far.at[1], down)]
        copies = [wire.put(to_up[1], at_up[1], up), wire.put(to_down[0], at_down[0], down)]
        yield
        first[0].wait_recv()
        to_up[0][...] += far[0]
        copies.append(wire.put(to_up[0], at_up[0], up))
        first[1].wait_recv()
        to_down[1][...] += far[1]
        copies.append(wire.put(to_down[1], at_down[1], down))
    yield
    arrive(copies)
    out[...] = pick(t)[...] + near[0] if n == 2 else pick(t)[...] + near[0] + near[1]


def gather_direct(me, wire, axis, pick):
    mine = pick(me.mine(axis))
    copies = [wire.put(mine, mine, me.along(axis, t)) for _, t in me.others(axis)]
    yield
    arrive(copies)


def reduce_direct(me, wire, axis, pick, near, out):
    copies = [wire.put(pick(t), near.at[o - 1], me.along(axis, t)) for o, t in me.others(axis)]
    yield
    arrive(copies)
    total = pick(me.mine(axis))[...]
    for o in range(me.side - 1):
        total = total + near[o]
    out[...] = total


def together(*parts):
    parts = list(parts)
    while parts:
        for part in list(parts):
            if next(part, parts) is parts:
                parts.remove(part)


def arrive(copies):
    for copy in copies:
        copy.wait_recv()


def hops(depth, layer):
    far, near = depth // 2, depth - 1 - depth // 2
    return (far, near) if layer % 2 == 0 else (near, far)


def staged(parts):
    while parts:
        for part in list(parts):
            if next(part, parts) is parts:
                parts.remove(part)
        if parts:
            yield


def eye_block():
    row = lax.broadcasted_iota(jnp.int32, (NB, NB), 0)
    return (row == lax.broadcasted_iota(jnp.int32, (NB, NB), 1)).astype(F32)


def take_block(ref, n):
    piece, side = ref.shape[-2], ref.shape[1]
    parts, done = [], 0
    while done < NB:
        index, offset = (n * NB + done) // piece, (n * NB + done) % piece
        rows = min(piece - offset, NB - done)
        parts.append(ref[index // (side * side), index // side % side, index % side, offset : offset + rows])
        done += rows
    return jnp.concatenate(parts, axis=0)


def place_block(ref, n, block):
    piece = ref.shape[-2]
    flat, side = n * NB, ref.shape[1]
    done = 0
    while done < NB:
        index, offset = (flat + done) // piece, (flat + done) % piece
        rows = min(piece - offset, NB - done)
        ref[index // (side * side), index // side % side, index % side, offset : offset + rows] = block[done : done + rows]
        done += rows


def leaf_inverse(x):
    groups = NB // 8
    rows = [x[8 * g : 8 * g + 8, :] for g in range(groups)]
    lane = lax.broadcasted_iota(jnp.int32, (8, NB), 1)
    sub = lax.broadcasted_iota(jnp.int32, (8, NB), 0)
    splat = lambda v, p: jnp.broadcast_to(v[p : p + 1, :], (8, NB))
    out = []
    for g in range(groups):
        base = 8 * g
        inside = (lane >= base) & (lane < base + 8)
        cur = rows[g]
        cols = [jnp.broadcast_to(cur[:, base + q : base + q + 1], (8, NB)) for q in range(8)]
        fwd = jnp.where(inside, jnp.where(lane == sub + base, 1.0, 0.0), cur)
        full = fwd
        last = (g + 1) % SPAN == 0
        for p in range(8):
            d = splat(cols[p], p)
            inv = 1.0 / d
            m = cols[p] * inv
            mf = jnp.where(sub > p, m, 0.0)
            pivot = d if p == 0 else jnp.where(sub == p, d, pivot)
            ipivot = inv if p == 0 else jnp.where(sub == p, inv, ipivot)
            if p < 7:
                fwd = fwd - mf * splat(fwd, p)
            if not last:
                mj = jnp.where(sub == p, 0.0, m)
                full = full - mj * splat(full, p)
            for q in range(p + 1, 8):
                cols[q] = cols[q] - (mf if last else mj) * splat(cols[q], p)
        y = fwd * lax.rsqrt(pivot)
        out.append(y)
        if last:
            if g + 1 < groups:
                first = g + 1 - SPAN
                block = jnp.concatenate(out[first : g + 1], axis=0)
                right = jnp.concatenate([jnp.where((lane >= 8 * f + 8) & (lane < base + 8), 0.0, out[f]) for f in range(first, g + 1)], axis=0)
                upd = lax.dot_general(block, right, (((0,), (0,)), ((), ())), precision=HI, preferred_element_type=F32)
                gone = (lane >= 8 * first) & (lane < base + 8)
                for i in range(g + 1, groups):
                    rows[i] = jnp.where(gone, 0.0, rows[i]) - upd[8 * i : 8 * i + 8, :]
        else:
            full = full * ipivot
            parts = [splat(full, q) for q in range(8)]
            for i in range(g + 1, g + 1 - (g + 1) % SPAN + SPAN):
                r = rows[i]
                acc = jnp.where(inside, 0.0, r)
                for q in range(8):
                    acc = acc - jnp.broadcast_to(r[:, base + q : base + q + 1], (8, NB)) * parts[q]
                rows[i] = acc
    return jnp.concatenate([jnp.where(lane < 8 * g + 8, y, 0.0) for g, y in enumerate(out)], axis=0)


def interleave(main, sides, turns):
    count = 0
    for _ in main:
        count += 1
        if count in turns:
            for side in sides:
                next(side, None)
    for side in sides:
        for _ in side:
            pass


def dion_kernel(layers, side, depth, q_ref, m_hbm, all_ref, rb_ref, s_ref, new_ref, m_ref, qall, part, chain, p_ref, pcore, a_ref, near_a, b_ref, near_b, t_ref, s3, g_ref, wall, rt, rc, far1, near1, u, near2, tot, sq, sz, qt, wt, send, recv, load):
    me = Place(side, depth)
    wire = Wire(send, recv)
    x, y, c, z = me.x, me.y, me.c, me.z
    rank = p_ref.shape[-1]
    rows = part.shape[2]
    width = m_ref.shape[-1]
    blocks = rank // NB
    loads = [pltpu.make_async_copy(m_hbm.at[l], m_ref.at[l], load.at[l]) for l in range(layers)]
    for copy in loads:
        copy.start()
    qall[:, x, y, c] = q_ref[...]
    me.barrier()

    def factor_rows(l):
        yield from gather_direct(me, wire, l, lambda t: qall.at[l, t, y, c] if l == 0 else qall.at[l, x, t, c])
        yield from gather_direct(me, wire, 1 - l, lambda t: qall.at[l, :, t, c] if l == 0 else qall.at[l, t, :, c])
        crossing.append(wire.put(qall.at[l, :, :, c], qall.at[l, :, :, c], me.at(c=1 - c)))

    crossing = []
    together(*[factor_rows(l) for l in range(layers)])

    right, left = lax.rem(z + 1, depth), lax.rem(z + depth - 1, depth)

    def chain_step(l, way, s):
        count = hops(depth, l)[way]
        ahead = count - s + 1
        dest = lax.rem(z + ahead, depth) if way == 0 else lax.rem(z + depth - ahead, depth)
        src = part.at[l, dest]
        if s > 1:
            src = chain.at[l, way, s - 2]
            src[...] += part[l, dest]
        return wire.put(src, chain.at[l, way, s - 1], me.at(z=right if way == 0 else left))

    pending = {}
    for l in range(layers):
        crossing[l].wait_recv()
        loads[l].wait()
        qt[...] = jnp.transpose(qall[l].reshape(rank, -1))

        @pl.loop(0, depth // 2)
        def _(i):
            lhs = m_ref[l, pl.ds(pl.multiple_of(i * 2 * rows, 16), 2 * rows), :]
            out = jnp.dot(lhs, qt[...], preferred_element_type=F32)
            part[l, pl.ds(2 * i, 2)] = out.reshape(2, rows, rank)

        for way in (0, 1):
            if hops(depth, l)[way]:
                pending[l, way] = chain_step(l, way, 1)
    for s in range(2, depth // 2 + 1):
        for l in range(layers):
            for way in (0, 1):
                if s <= hops(depth, l)[way]:
                    pending[l, way].wait_recv()
                    pending[l, way] = chain_step(l, way, s)
    for l in range(layers):
        total = part[l, z]
        for way in (0, 1):
            count = hops(depth, l)[way]
            if count:
                pending[l, way].wait_recv()
                total = total + chain[l, way, count - 1]
        p_ref[l, z] = total

    def gather_project(l):
        pending = {}
        for s in range(1, depth // 2 + 1):
            for way in (0, 1):
                if s <= hops(depth, l)[way]:
                    if s > 1:
                        pending[way].wait_recv()
                    src = lax.rem(z + depth - (s - 1), depth) if way == 0 else lax.rem(z + s - 1, depth)
                    block = p_ref.at[l, src]
                    pending[way] = wire.put(block, block, me.at(z=right if way == 0 else left))
            yield
        arrive(list(pending.values()))

    def sum_plane(h):
        yield from reduce_direct(me, wire, h, lambda t: a_ref.at[h, t], near_a.at[h], b_ref.at[h])
        yield from reduce_direct(me, wire, 1 - h, lambda t: b_ref.at[h, t], near_b.at[h], t_ref.at[h])

    def spread_plane(h):
        i = me.mine(h)
        yield from gather_direct(me, wire, 1 - h, lambda t: g_ref.at[h, i, t])
        yield from gather_direct(me, wire, h, lambda t: g_ref.at[h, t])

    def sum_gram_and_invert():
        swap = wire.put(p_ref.at[1 - c, z], pcore, me.at(c=1 - c))
        for l in range(layers):
            next(sides[l])
        swap.wait_recv()
        both = jnp.concatenate([p_ref[c, z], pcore[...]], axis=0)
        n = 0
        for i in range(blocks):
            gram = lax.dot_general(both[:, i * NB : i * NB + NB], both[:, i * NB :], (((0,), (0,)), ((), ())), precision=HI, preferred_element_type=F32)
            for j in range(blocks - i):
                place_block(a_ref, n, gram[:, j * NB : j * NB + NB])
                n += 1
        yield from staged([sum_plane(0), sum_plane(1)])
        copies = [wire.put(t_ref, s3.at[o - 1], me.at(z=t)) for o, t in me.others_z()]
        yield
        arrive(copies)
        total = t_ref[...]
        for o in range(depth - 1):
            total = total + s3[o]
        for h in (0, 1):
            g_ref[h, me.mine(h), me.mine(1 - h)] = total[h]
        yield from staged([spread_plane(0), spread_plane(1)])
        wall[c] = jnp.zeros(wall.shape[1:], F32)
        n = 0
        for i in range(blocks):
            for j in range(i, blocks):
                wall[c, i * NB : i * NB + NB, j * NB : j * NB + NB] = take_block(g_ref, n)
                n += 1
        ident = eye_block()
        for k in range(blocks):
            yield
            sl = slice(k * NB, k * NB + NB)
            w = leaf_inverse(wall[c, sl, sl])
            colid = lax.broadcasted_iota(jnp.int32, (NB, rank), 1) // NB
            row = jnp.where(colid == k, jnp.concatenate([ident] * blocks, axis=1), wall[c, sl, :])
            out = jnp.dot(w, row, precision=HI, preferred_element_type=F32)
            wall[c, sl, :] = jnp.where(colid <= k, out, 0.0)
            if k + 1 < blocks:
                tail = slice(k * NB + NB, rank)
                upd = lax.dot_general(out[:, k * NB + NB :], out, (((0,), (0,)), ((), ())), precision=HI, preferred_element_type=F32)
                keep = wall[c, tail, :]
                cid = lax.broadcasted_iota(jnp.int32, keep.shape, 1) // NB
                wall[c, tail, :] = jnp.where(cid == k, 0.0, keep) - upd

    sides = [gather_project(l) for l in range(layers)]
    interleave(sum_gram_and_invert(), sides, (3, 5, 7))
    wire.put(wall.at[c], wall.at[c], me.at(c=1 - c)).wait_recv()

    def sum_rows(l):
        core = wire.put(rt.at[l, :, :, 1 - c], rc.at[l], me.at(c=1 - c))
        yield
        core.wait_recv()
        rc[l] += rt[l, :, :, c]
        pick = lambda t: rc.at[l, t] if l == 0 else rc.at[l, :, t]
        yield from reduce_ring(me, wire, l, pick, far1.at[l], near1.at[l], u.at[l])
        yield from reduce_direct(me, wire, 1 - l, lambda t: u.at[l, t], near2.at[l], tot.at[l])

    sums = []
    for l in range(layers):
        turned = jnp.transpose(wall[l])
        wt[0] = turned.astype(BF16)
        wt[1] = (turned - turned.astype(BF16).astype(F32)).astype(BF16)

        @pl.loop(0, depth // 2)
        def _(i):
            lhs = p_ref[l, pl.ds(2 * i, 2)].reshape(-1, rank)
            high = lhs.astype(BF16)
            low = (lhs - high.astype(F32)).astype(BF16)
            dot = lambda a, b: jnp.dot(a, b, preferred_element_type=F32)
            out = dot(high, wt[0]) + (dot(high, wt[1]) + dot(low, wt[0]))
            all_ref[l, pl.ds(2 * i, 2)] = out.astype(BF16).reshape(2, -1, rank)

        for part_sum in sums:
            next(part_sum)
        ortho = all_ref[l].reshape(-1, rank)
        for k in range(width // 256):
            cols = slice(256 * k, 256 * k + 256)
            out = lax.dot_general(ortho, m_ref[l, :, cols], (((0,), (0,)), ((), ())), preferred_element_type=F32)
            rt[l, :, :, :, :, cols] = out.reshape(rt.shape[1:5] + (256,))
        sums.append(sum_rows(l))
        next(sums[l])
    together(*sums)

    def gather_rows(l):
        rb_ref[l, x, y, c] = tot[l].astype(BF16)
        yield from gather_direct(me, wire, l, lambda t: rb_ref.at[l, t, y, c] if l == 0 else rb_ref.at[l, x, t, c])
        yield from gather_direct(me, wire, 1 - l, lambda t: rb_ref.at[l, :, t, c] if l == 0 else rb_ref.at[l, t, :, c])
        cross = wire.put(rb_ref.at[l, :, :, c], rb_ref.at[l, :, :, c], me.at(c=1 - c))
        yield
        cross.wait_recv()

    def gather_norms():
        for l in range(layers):
            sq[l] = jnp.broadcast_to(jnp.sum(tot[l] * tot[l], axis=1, keepdims=True), sq.shape[1:])
        copies = [wire.put(sq, sz.at[o - 1], me.at(z=t)) for o, t in me.others_z()]
        yield
        arrive(copies)
        norm = sq[...]
        for o in range(depth - 1):
            norm = norm + sz[o]
        factor = lax.rsqrt(norm + 1e-06)
        for l in range(layers):
            s_ref[l, x, y, c] = factor[l]
            new_ref[l] = (tot[l] * factor[l, :, :1]).astype(BF16)
        mine = s_ref.at[:, x, y, c]
        copies = [wire.put(mine, mine, me.along(0, t)) for _, t in me.others(0)]
        yield
        arrive(copies)
        mine = s_ref.at[:, :, y, c]
        copies = [wire.put(mine, mine, me.along(1, t)) for _, t in me.others(1)]
        yield
        arrive(copies)
        copies = [wire.put(s_ref.at[:, :, :, c], s_ref.at[:, :, :, c], me.at(c=1 - c))]
        yield
        arrive(copies)

    together(gather_norms(), *[gather_rows(l) for l in range(layers)])
    wire.finish()


def dion(momentum, factor, side, depth):
    layers, rows, width = momentum.shape
    per = factor.shape[1]
    rank = per * side * side * CORES
    short = rows // depth
    blocks = rank // NB
    piece = blocks * (blocks + 1) // 2 * NB // (2 * side * side)
    whole = (2, side, side, piece, NB)
    grid = (side, side, CORES, per)
    ortho, rb, s, new = pl.pallas_call(
        functools.partial(dion_kernel, layers, side, depth),
        out_shape=(
            jax.ShapeDtypeStruct((layers, depth, short, rank), BF16),
            jax.ShapeDtypeStruct((layers,) + grid + (width,), BF16),
            jax.ShapeDtypeStruct((layers,) + grid + (128,), F32),
            jax.ShapeDtypeStruct((layers, per, width), BF16),
        ),
        in_specs=[pl.BlockSpec(memory_space=pltpu.VMEM), pl.BlockSpec(memory_space=pl.ANY)],
        out_specs=[pl.BlockSpec(memory_space=pltpu.VMEM)] * 4,
        scratch_shapes=[
            pltpu.VMEM(momentum.shape, BF16),
            pltpu.VMEM((layers,) + grid + (width,), BF16),
            pltpu.VMEM((layers, depth, short, rank), F32),
            pltpu.VMEM((layers, 2, max(1, depth // 2), short, rank), F32),
            pltpu.VMEM((layers, depth, short, rank), F32),
            pltpu.VMEM((short, rank), F32),
            pltpu.VMEM(whole, F32),
            pltpu.VMEM((2, side - 1) + whole[2:], F32),
            pltpu.VMEM((2,) + whole[2:], F32),
            pltpu.VMEM((2, side - 1) + whole[3:], F32),
            pltpu.VMEM((2,) + whole[3:], F32),
            pltpu.VMEM((depth - 1, 2) + whole[3:], F32),
            pltpu.VMEM(whole, F32),
            pltpu.VMEM((layers, rank, rank), F32),
            pltpu.VMEM((layers,) + grid + (width,), F32),
            pltpu.VMEM((layers, side, side, per, width), F32),
            pltpu.VMEM((layers, 2, side, per, width // 2), F32),
            pltpu.VMEM((layers, 2, side, per, width), F32),
            pltpu.VMEM((layers, side, per, width), F32),
            pltpu.VMEM((layers, side - 1, per, width), F32),
            pltpu.VMEM((layers, per, width), F32),
            pltpu.VMEM((layers, per, 128), F32),
            pltpu.VMEM((depth - 1, layers, per, 128), F32),
            pltpu.VMEM((width, rank), BF16),
            pltpu.VMEM((2, rank, rank), BF16),
            pltpu.SemaphoreType.DMA((160,)),
            pltpu.SemaphoreType.DMA((160,)),
            pltpu.SemaphoreType.DMA((layers,)),
        ],
        compiler_params=pltpu.CompilerParams(collective_id=0, has_side_effects=True, vmem_limit_bytes=VMEM_BYTES),
        name="dion",
    )(factor, momentum)
    return ortho.reshape(layers, rows, rank), rb.reshape(layers, rank, width), s.reshape(layers, rank, 128), new


def final_kernel(scale, o_ref, m_ref, rb_ref, s_ref, mom_ref, up_ref):
    ortho, rb = o_ref[0], rb_ref[0]
    feedback = jnp.dot(ortho, rb, preferred_element_type=F32)
    mom_ref[0] = (m_ref[0].astype(F32) - 0.05 * feedback).astype(BF16)
    normed = (rb.astype(F32) * s_ref[0, :, :1]).astype(BF16)
    up_ref[0] = (scale * jnp.dot(ortho, normed, preferred_element_type=F32)).astype(BF16)


def final_products(ortho, momentum, rb, s, scale):
    layers, rows, rank = ortho.shape
    width = momentum.shape[-1]
    block = rows // 2
    tall = lambda w: pl.BlockSpec((1, block, w), lambda l, i: (l, i, 0))
    full = lambda w: pl.BlockSpec((1, rank, w), lambda l, i: (l, 0, 0))
    return pl.pallas_call(
        functools.partial(final_kernel, scale),
        grid=(layers, 2),
        out_shape=[jax.ShapeDtypeStruct(momentum.shape, BF16)] * 2,
        in_specs=[tall(rank), tall(width), full(width), full(128)],
        out_specs=[tall(width)] * 2,
        compiler_params=pltpu.CompilerParams(vmem_limit_bytes=VMEM_BYTES),
        name="final_products",
    )(ortho, momentum, rb, s)


def solution(mesh):
    side = math.isqrt(mesh.shape["fsdp"] // CORES)
    depth = mesh.shape["tp"]

    def local(momentum, right_factor):
        rank = right_factor.shape[1] * side * side * CORES
        total_rows, total_cols = momentum.shape[1] * side * side * CORES, momentum.shape[2] * depth
        scale = math.sqrt(total_rows * total_cols / rank)
        ortho, rb, s, new_factor = dion(momentum, right_factor, side, depth)
        new_momentum, update = final_products(ortho, momentum, rb, s, scale)
        return new_momentum, update, new_factor

    spec = P(None, "fsdp", "tp")
    return jax.shard_map(local, mesh=mesh, in_specs=(spec, spec), out_specs=(spec, spec, spec), check_vma=False)
```
